32 devices in a mesh: mode: 4 (over y, core), mesh: 8 (over z, x).
Axes of the slice: x: 2, y: 2, z: 4, core: 2. Of those that a mesh axis runs over, the one named last changes fastest.
Arguments:
- src_rows: bfloat16 [8192, 640], P(('mode', 'mesh')), parts along dimension 0, may hold values from -4 to 4
- src_owner: int32 [8192, 1], P(('mode', 'mesh')), parts along dimension 0, may hold values from 0 to 7; in each aligned block of 256 rows (0 to 255, 256 to 511, ...) at most 64 rows name the same one
- src_slot: int32 [8192], P(('mode', 'mesh')), parts along dimension 0, may hold values from 0 to 63
- neighbour_offset: int32 [2048, 6], P(('mode', 'mesh')), parts along dimension 0, may hold values from -16 to 16
- liner_face: int32 [2048], P(('mode', 'mesh')), parts along dimension 0, may hold values from 0 to 127
- admittance: float32 [8, 128], P('mode', 'mesh'), parts along dimension 0, may hold values from 0.2 to 1.5
- observe_weight: float32 [2048], P(('mode', 'mesh')), parts along dimension 0, may hold values from 0.3 to 3
- coupling: bfloat16 [24, 320, 640], P('mode'), parts along dimension 0, may hold values from -0.046875 to 0.046875
- block_inv: bfloat16 [1280, 640], P('mode'), parts along dimension 0, may hold values from -1.5 to 1.5, as said below
- liner_op: bfloat16 [1280, 640], P('mode'), parts along dimension 0, may hold values from -0.0625 to 0.0625
Outputs:
- state_field: bfloat16 [2048, 640], P(('mode', 'mesh')), parts along dimension 0
- adjoint_field: bfloat16 [2048, 640], P(('mode', 'mesh')), parts along dimension 0
- liner_grad: float32 [8, 128], P('mode', 'mesh'), parts along dimension 0
The draws below stay inside these ranges and needn't reach their ends.
There are 4 independent parts, one for each index of `mode`. The reference program is written for one: setup_inputs(seed, part) draws one part's arguments, and reference() takes and returns one part's arrays. A program takes and returns all parts, laid end to end along the dimension named above; each array names one. Nothing has to cross between parts.
Inputs may be any that keep to these rules, and one draw needn't show every extreme that they name: `src_owner`: in the rows of one device no owner is named by more than 64 rows, a bound that some block reaches. `block_inv`: real parts of the diagonal entries lie near 0.8; the rest is of order 320 ** -0.5.
All inputs are finite; a program needn't handle non-finite values.
Results may differ from the reference program's by a relative error of at most 0.018.
Values may be sent and summed in bfloat16 or wider, within the bound.
A program may use at most 64 MiB of HBM per device.

```python
import math
import jax
import jax.numpy as jnp
import numpy as np
from jax import lax

NB = 320
EL_DEV = 64
RIM = 16
SRC_DEV = 256
SWEEPS = 4
CAP = 64
ELEMS = 512
SOURCES = 2048
LFACES = 128
N_MESH = 8


def draw_block_inv(key, part):
    key_noise = jax.random.fold_in(key, 17)
    jitter = jnp.clip(jax.random.normal(key_noise, (NB, 2 * NB), jnp.float32), -4.0, 4.0)
    identity = jnp.concatenate([jnp.eye(NB, dtype=jnp.float32), jnp.zeros((NB, NB), jnp.float32)], axis=1)
    return (0.8 * identity + 0.6 / NB ** 0.5 * jitter).astype(jnp.bfloat16)


def touch_ends(entries, stream_key, low, largest):
    spot = [jax.random.randint(jax.random.fold_in(stream_key, axis), (), 0, length) for axis, length in enumerate(entries.shape)]
    longest = entries.shape.index(max(entries.shape))
    next_to = spot[:longest] + [(spot[longest] + 1) % entries.shape[longest]] + spot[longest + 1:]
    return entries.at[tuple(spot)].set(low).at[tuple(next_to)].set(largest)


def shard_levels(own_key, shape, cuts, least, top_value):
    level, own = 1.0, jax.random.fold_in(own_key, 6)
    for position, shards_of in cuts:
        heights = jnp.exp(jax.random.uniform(jax.random.fold_in(own, position), (shards_of,), jnp.float32, least / len(cuts), top_value / len(cuts)))
        level = level * jnp.repeat(heights, shape[position] // shards_of).reshape([-1 if axis == position else 1 for axis in range(len(shape))])
    return level


def routed_block(rng, own, number, rows, count, top, bound, lean):
    order = jax.random.permutation(rng, count)
    heavy_load, ordinary = load_shares(count, rows * top, bound, lean, True), load_shares(count, rows * top, bound, lean, False)
    places = jnp.arange(count)

    def named(tallies, offset_by):
        used = int((tallies > 0).sum())
        fixed = max(1, used // 4)
        moved = fixed + (places - fixed + offset_by * (used - fixed)) % max(1, count - fixed)
        return jnp.zeros((count,), jnp.int32).at[order[jnp.where(places < fixed, places, moved)]].set(jnp.asarray(tallies, jnp.int32))

    tallies = jnp.where(number % 4 == 0, named(heavy_load, number // 4), named(ordinary, number - number // 4 - 1))
    mixed = jax.random.permutation(jax.random.fold_in(own, 3), count)
    source_of, taker = mixed[0:count // 2 * 2:2], mixed[1:count // 2 * 2:2]
    margin = jnp.minimum(tallies[source_of] - 1, bound - tallies[taker]) // 2
    margin = jnp.where((source_of == order[0]) | (taker == order[0]) | (tallies[taker] == 0), 0, jnp.maximum(margin, 0))
    moved = jax.random.randint(jax.random.fold_in(own, 4), (count // 2,), 0, 1 << 20) % (margin + 1)
    tallies = tallies.at[source_of].add(-moved).at[taker].add(moved)
    members = jnp.searchsorted(jnp.cumsum(tallies), jnp.arange(rows * top), side="right").astype(jnp.int32)
    grid = members.reshape(top, rows).T
    grid = grid[jax.random.permutation(jax.random.fold_in(own, 1), rows)]
    offset_by = jax.random.randint(jax.random.fold_in(own, 2), (rows, 1), 0, top)
    return jnp.take_along_axis(grid, (jnp.arange(top)[None, :] + offset_by) % top, axis=1)


def load_shares(amount, total, bound, skew, full):
    weights = [(1 << 20) // math.isqrt(grade ** skew) + 1 for grade in range(1, amount + 1)]
    largest = bound if full else min(bound, max(-(-total // amount), total * weights[0] // sum(weights)))
    least = 1 if total - largest >= amount - 1 else 0
    counts, spare = [largest] + [least] * (amount - 1), total - largest - least * (amount - 1)
    while spare > 0:
        free = [i for i in range(1, amount) if counts[i] < largest] or [i for i in range(1, amount) if counts[i] < bound]
        pool, budget = sum([weights[i] for i in free]), spare
        for i in free:
            more = min(bound - counts[i], max(1, budget * weights[i] // pool), spare)
            counts[i] = counts[i] + more
            spare = spare - more
    return np.array(counts)


def scatter_about(rng, dims, scale, bound, split=(), held_as=jnp.bfloat16):
    gain = shard_levels(rng, dims, split, -0.22, 0.18) if split else 1.0
    result = jax.random.normal(rng, dims, jnp.float32) * scale * gain
    return jnp.minimum(jnp.maximum(result, -bound), bound).astype(held_as)


def setup_inputs(seed: int = 0, part: int = 0) -> dict:
    arg_keys = jax.random.split(jax.random.key(seed), 11)
    own_keys = jax.random.split(jax.random.fold_in(arg_keys[10], part), 11)
    src_rows = scatter_about(own_keys[0], (SOURCES, 2 * NB), 0.5, 4.0, ((0, 8),))
    src_owner_keys = jax.random.split(jax.random.fold_in(own_keys[1], 1), SOURCES // SRC_DEV)
    src_owner_turns = jax.random.permutation(jax.random.fold_in(own_keys[1], 3), SOURCES // SRC_DEV)
    src_owner = jax.vmap(lambda own, number: routed_block(jax.random.fold_in(own_keys[1], 2), own, number, SRC_DEV, N_MESH, 1, CAP, 2))(src_owner_keys, src_owner_turns).reshape((SOURCES, 1))
    src_slot = touch_ends(jax.random.randint(own_keys[2], (SOURCES,), 0, EL_DEV), jax.random.fold_in(own_keys[2], 1), 0, EL_DEV - 1).astype(jnp.int32)
    neighbour_offset = touch_ends(jax.random.randint(own_keys[3], (ELEMS, 6), -RIM, RIM + 1), jax.random.fold_in(own_keys[3], 1), -RIM, RIM).astype(jnp.int32)
    liner_face = touch_ends(jax.random.randint(own_keys[4], (ELEMS,), 0, LFACES), jax.random.fold_in(own_keys[4], 1), 0, LFACES - 1).astype(jnp.int32)
    admittance = jnp.clip(0.2 + 1.3 * jax.random.uniform(own_keys[5], (2, LFACES), jnp.float32) ** shard_levels(own_keys[5], (2, LFACES), ((1, 8),), -0.2, 0.2), 0.2, 1.5)
    observe_weight = jnp.clip(jnp.exp(math.log(3.0) - 2.3025851 * jax.random.uniform(own_keys[6], (ELEMS,), jnp.float32) ** shard_levels(own_keys[6], (ELEMS,), ((0, 8),), -0.2, 0.2)), 0.3, 3.0)
    coupling = scatter_about(own_keys[7], (6, NB, 2 * NB), (48 * NB) ** -0.5, 0.046875)
    block_inv = draw_block_inv(jax.random.fold_in(jax.random.fold_in(arg_keys[10], part), 71), part)
    liner_op = scatter_about(own_keys[9], (NB, 2 * NB), (32 * NB) ** -0.5, 0.0625)
    return {"src_rows": src_rows, "src_owner": src_owner, "src_slot": src_slot, "neighbour_offset": neighbour_offset, "liner_face": liner_face, "admittance": admittance, "observe_weight": observe_weight, "coupling": coupling, "block_inv": block_inv, "liner_op": liner_op}


def complex_apply(rows_in, matrix):
    half_width = matrix.shape[0]
    row_count = rows_in.shape[0]
    stacked = jnp.concatenate([rows_in[:, :half_width], rows_in[:, half_width:]], axis=0)
    product = jnp.dot(stacked, matrix, preferred_element_type=jnp.float32)
    upper_half = product[:row_count]
    lower_half = product[row_count:]
    return jnp.concatenate([upper_half[:, :half_width] - lower_half[:, half_width:], upper_half[:, half_width:] + lower_half[:, :half_width]], axis=1)


def hermitian_apply(rows_in, matrix):
    half_width = matrix.shape[0]
    row_count = rows_in.shape[0]
    swapped = jnp.concatenate([rows_in[:, half_width:], -rows_in[:, :half_width]], axis=1)
    stacked = jnp.concatenate([rows_in, swapped], axis=0)
    product = lax.dot_general(stacked, matrix, (((1,), (1,)), ((), ())), preferred_element_type=jnp.float32)
    return jnp.concatenate([product[:row_count], product[row_count:]], axis=1)


def wall_term(wall_wave, resist, reactance, conjugate):
    half_width = wall_wave.shape[1] // 2
    real_part = wall_wave[:, :half_width]
    imag_part = wall_wave[:, half_width:]
    sign_value = -1.0 if conjugate else 1.0
    resist = resist[:, None]
    reactance = sign_value * reactance[:, None]
    return jnp.concatenate([resist * real_part - reactance * imag_part, resist * imag_part + reactance * real_part], axis=1)


def reference(src_rows, src_owner, src_slot, neighbour_offset, liner_face, admittance, observe_weight, coupling, block_inv, liner_op):
    elem_total = EL_DEV * N_MESH
    target = (src_owner[:, 0] * EL_DEV + src_slot).astype(jnp.int32)
    forcing = jnp.zeros((elem_total, 2 * NB), jnp.float32).at[target].add(src_rows.astype(jnp.float32))
    resist = jnp.take(admittance[0], liner_face)
    reactance = jnp.take(admittance[1], liner_face)
    face_index = (jnp.arange(elem_total, dtype=jnp.int32)[:, None] + RIM + neighbour_offset).astype(jnp.int32)
    state_field = complex_apply(forcing.astype(jnp.bfloat16), block_inv).astype(jnp.bfloat16)
    for sweep_step in range(SWEEPS):
        padded = jnp.pad(state_field, ((RIM, RIM), (0, 0)))
        residual_sum = forcing - wall_term(complex_apply(state_field, liner_op), resist, reactance, False)
        for face_dir in range(6):
            residual_sum = residual_sum - complex_apply(jnp.take(padded, face_index[:, face_dir], axis=0), coupling[face_dir])
        state_field = complex_apply(residual_sum.astype(jnp.bfloat16), block_inv).astype(jnp.bfloat16)
    source = observe_weight[:, None] * state_field.astype(jnp.float32)
    adjoint_field = hermitian_apply(source.astype(jnp.bfloat16), block_inv).astype(jnp.bfloat16)
    for sweep_step in range(SWEEPS):
        spread = jnp.zeros((elem_total + 2 * RIM, 2 * NB), jnp.float32)
        for face_dir in range(6):
            spread = spread.at[face_index[:, face_dir]].add(hermitian_apply(adjoint_field, coupling[face_dir]))
        residual_sum = source - spread[RIM:RIM + elem_total] - wall_term(hermitian_apply(adjoint_field, liner_op), resist, reactance, True)
        adjoint_field = hermitian_apply(residual_sum.astype(jnp.bfloat16), block_inv).astype(jnp.bfloat16)
    wall_wave = complex_apply(state_field, liner_op)
    adjoint_f = adjoint_field.astype(jnp.float32)
    term_re = -jnp.sum(adjoint_f[:, :NB] * wall_wave[:, :NB] + adjoint_f[:, NB:] * wall_wave[:, NB:], axis=1) / 16.0
    term_im = -jnp.sum(adjoint_f[:, NB:] * wall_wave[:, :NB] - adjoint_f[:, :NB] * wall_wave[:, NB:], axis=1) / 16.0
    liner_grad = jnp.zeros((2, LFACES), jnp.float32)
    liner_grad = liner_grad.at[0, liner_face].add(term_re).at[1, liner_face].add(term_im)
    return state_field, adjoint_field, liner_grad
```

```python
import functools

import jax
import jax.numpy as jnp
from jax import lax
from jax.experimental import pallas as pl
from jax.experimental.pallas import tpu as pltpu
from jax.sharding import PartitionSpec as P

SWEEPS = 4
RIM = 16
DEEP = 2 * RIM
FACES = 6
HALF = 384
FULL = 2 * HALF
MESH = pl.DeviceIdType.MESH
F32 = jnp.float32
BF16 = jnp.bfloat16


def iota(shape, dim):
    return lax.broadcasted_iota(jnp.int32, shape, dim)


def dot(a, b):
    return jnp.dot(a, b, preferred_element_type=F32)


def widen(x, nb):
    rows = x.shape[0]
    turned = pltpu.roll(x, HALF - nb, 1)
    wrap = 2 * (HALF - nb)
    real = jnp.where(iota((rows, HALF), 1) < nb, x[:, :HALF], 0.0)
    last = jnp.where(iota((rows, wrap), 1) < HALF - nb, turned[:, :wrap], 0.0)
    return jnp.concatenate([real, turned[:, HALF:], last], axis=1)


def narrow(x, nb):
    turned = pltpu.roll(x, FULL - (HALF - nb), 1)
    return jnp.where(iota((x.shape[0], 2 * nb), 1) < nb, x[:, : 2 * nb], turned[:, : 2 * nb])


def combine(prod):
    rows = prod.shape[0] // 2
    return (
        prod[:rows, :HALF] - prod[rows:, HALF:],
        prod[:rows, HALF:] + prod[rows:, :HALF],
    )


def halves(x):
    return jnp.concatenate([x[:, :HALF], x[:, HALF:]], axis=0)


def column(row):
    count = row.shape[1]
    same = iota((count, count), 0) == iota((count, count), 1)
    return jnp.sum(jnp.where(same, row, 0.0), axis=1, keepdims=True)


def kernel(
    n,
    owner_ref,
    slot_ref,
    off_ref,
    face_ref,
    adm_ref,
    weight_ref,
    src_ref,
    coupling_hbm,
    inv_hbm,
    liner_hbm,
    state_ref,
    adjoint_ref,
    grad_ref,
    send,
    recv,
    adm_send,
    adm_recv,
    off_send,
    off_halo,
    grad_send,
    grad_recv,
    fields,
    w_fwd,
    w_adj,
    inv_pad,
    inv_herm,
    liner_pad,
    matrix,
    pick_fwd,
    pick_adj,
    src_sems,
    adm_sems,
    off_sems,
    grad_sems,
    halo_sems,
    coupling_ref,
    inv_ref,
    liner_ref,
    load_sems,
):
    me = lax.axis_index("mesh")
    elems = off_ref.shape[1]
    nb = inv_ref.shape[0]
    lin = adm_ref.shape[1]
    rows = src_ref.shape[0]

    loads = [
        pltpu.make_async_copy(hbm, here, load_sems.at[i])
        for i, (hbm, here) in enumerate(
            ((inv_hbm, inv_ref), (liner_hbm, liner_ref), (coupling_hbm, coupling_ref))
        )
    ]
    for load in loads:
        load.start()

    def peer(k):
        return lax.rem(me + k, n)

    def to(src, dst, send_sem, recv_sem, p):
        return pltpu.make_async_remote_copy(
            src_ref=src,
            dst_ref=dst,
            send_sem=send_sem,
            recv_sem=recv_sem,
            device_id={"mesh": p},
            device_id_type=MESH,
        )

    def src_copy(p, owner):
        return to(send.at[p], recv.at[owner], src_sems.at[0, p], src_sems.at[1, owner], p)

    def adm_copy(p, owner):
        return to(adm_send, adm_recv.at[owner], adm_sems.at[0, p], adm_sems.at[1, owner], p)

    def grad_copy(p, owner):
        return to(
            grad_send.at[p], grad_recv.at[owner], grad_sems.at[0, p], grad_sems.at[1, owner], p
        )

    def off_copy(side, p):
        return to(off_send, off_halo.at[side], off_sems.at[0, side], off_sems.at[1, side], p)

    def halo_copy(step, side, p):
        own = pl.ds(elems - DEEP if side == 0 else 0, DEEP)
        there = pl.ds(elems if side == 0 else elems + DEEP, DEEP)
        return to(
            fields.at[step, own],
            fields.at[step, there],
            halo_sems.at[0, step // 2, side],
            halo_sems.at[1, step // 2, side],
            p,
        )

    up, down = jnp.minimum(me + 1, n - 1), jnp.maximum(me - 1, 0)
    has_up, has_down = me < n - 1, me > 0

    fields[...] = jnp.zeros_like(fields)
    off_halo[...] = jnp.zeros_like(off_halo)

    barrier = pltpu.get_barrier_semaphore()

    @pl.loop(1, n)
    def _(k):
        pl.semaphore_signal(barrier, inc=1, device_id={"mesh": peer(k)}, device_id_type=MESH)

    adm_send[...] = jnp.zeros_like(adm_send)
    adm_send[0:2, 0:lin] = adm_ref[...]
    off_send[...] = jnp.zeros_like(off_send)
    off_send[0:FACES, 0:elems] = off_ref[...].astype(F32)
    off_send[FACES : FACES + 1, 0:elems] = face_ref[...].astype(F32)
    target = owner_ref[...] * elems + slot_ref[...]

    def partial_sum(p):
        pick = (iota((elems, rows), 0) + p * elems) == target
        return dot(pick.astype(F32).astype(BF16), src_ref[...])

    @pl.loop(1, n)
    def _(k):
        p = peer(k)
        send[p] = partial_sum(p).astype(BF16)

    pl.semaphore_wait(barrier, n - 1)

    @pl.loop(1, n)
    def _(k):
        src_copy(peer(k), me).start()

    @pl.when(has_up)
    def _():
        off_copy(0, up).start()

    @pl.when(has_down)
    def _():
        off_copy(1, down).start()

    @pl.loop(1, n)
    def _(k):
        adm_copy(peer(k), me).start()

    def padded(x):
        wide = widen(x.astype(F32), nb)
        return jnp.concatenate([wide, jnp.zeros((HALF - nb, FULL), F32)], axis=0)

    for load in loads:
        load.wait()
    inv_wide = padded(inv_ref[...])
    inv_pad[...] = inv_wide.astype(BF16)
    inv_herm[:, :HALF] = inv_wide[:, :HALF].T.astype(BF16)
    inv_herm[:, HALF:] = (-inv_wide[:, HALF:].T).astype(BF16)
    liner_pad[...] = padded(liner_ref[...]).astype(BF16)

    def fold(f):
        at = pl.ds(pl.multiple_of(f * HALF, HALF), HALF)
        re, im = combine(dot(halves(matrix[...]), inv_pad[...]))
        w_fwd[at, :HALF] = re.astype(BF16)
        w_fwd[at, HALF:] = im.astype(BF16)
        re, im = combine(dot(halves(inv_pad[...]), matrix[...]))
        w_adj[at, :HALF] = re.T.astype(BF16)
        w_adj[at, HALF:] = (-im.T).astype(BF16)

    @pl.loop(0, FACES)
    def _(f):
        matrix[...] = padded(coupling_ref[f]).astype(BF16)
        fold(f)

    matrix[...] = liner_pad[...]
    fold(FACES)

    @pl.when(has_down)
    def _():
        off_copy(0, down).wait_recv()

    @pl.when(has_up)
    def _():
        off_copy(1, up).wait_recv()

    lane8 = iota((8, 128), 1)
    offs = jnp.where(
        lane8 < elems,
        off_send[...],
        jnp.where(
            lane8 < elems + DEEP,
            pltpu.roll(off_halo[0], DEEP, 1),
            pltpu.roll(off_halo[1], elems + DEEP, 1),
        ),
    )
    lane = iota((128, 128), 1)
    place_row = jnp.where(
        lane < elems, lane, jnp.where(lane < elems + DEEP, lane - elems - DEEP, lane - DEEP)
    ).astype(F32)
    place_col = place_row.T
    near = elems + DEEP - RIM

    def kept(x):
        return jnp.concatenate([x[:elems], x[near : near + DEEP]], axis=0)

    for f in range(FACES):
        lands = jnp.where(place_col == place_row + offs[f : f + 1, :], 1.0, 0.0)
        pick_adj[f] = kept(lands).astype(BF16)
        pick_fwd[f] = kept(lands.T).astype(BF16)

    face_all = kept(column(offs[FACES : FACES + 1, :]))
    face = face_all[:elems]
    weight = column(weight_ref[...])
    lane_e = iota((elems, 128), 1)

    lane_a = iota((elems + DEEP, 128), 1)

    def face_pick(p):
        return jnp.logical_and(face == (lane_e + p * lin).astype(F32), lane_e < lin)

    def admit(table, p, sums):
        pick = jnp.logical_and(face_all == (lane_a + p * lin).astype(F32), lane_a < lin)
        return tuple(s + jnp.where(pick, table[i : i + 1, :], 0.0) for i, s in enumerate(sums))

    def admit_peer(k, sums):
        p = peer(n - k)
        adm_copy(p, p).wait_recv()
        return admit(adm_recv[p], p, sums)

    sums = admit(adm_send[...], me, (jnp.zeros((elems + DEEP, 128), F32),) * 2)
    sums = lax.fori_loop(1, n, admit_peer, sums)
    y_re = jnp.sum(sums[0], axis=1, keepdims=True)
    y_im = jnp.sum(sums[1], axis=1, keepdims=True)

    def take(k, total):
        p = peer(n - k)
        src_copy(p, p).wait_recv()
        return total + recv[p].astype(F32)

    forcing = widen(lax.fori_loop(1, n, take, partial_sum(me)), nb)

    def sweeps(first, start, pick_ref, w_ref, yi, beside):
        def sweep(s, pick, u, y_r, y_i):
            count = u.shape[0]
            u_re, u_im = u[:, :HALF], u[:, HALF:]
            wall = jnp.concatenate([y_r * u_re - y_i * u_im, y_r * u_im + y_i * u_re], axis=0)
            met = dot(pick.reshape(FACES * count, 128), fields[s]).astype(BF16)
            parts = [halves(met[f * count : (f + 1) * count]) for f in range(FACES)]
            left = jnp.concatenate(parts + [wall.astype(BF16)], axis=1)
            return jnp.concatenate(combine(dot(left, w_ref[...])), axis=1)

        start = jnp.concatenate(start, axis=1)
        now = start.astype(BF16)
        start_near = None
        for s in range(first, first + SWEEPS, 2):
            fields[s, 0:elems, :] = now

            @pl.when(has_up)
            def _():
                halo_copy(s, 0, up).start()

            @pl.when(has_down)
            def _():
                halo_copy(s, 1, down).start()

            if s == first:
                beside()

            @pl.when(has_down)
            def _():
                halo_copy(s, 0, down).wait_recv()

            @pl.when(has_up)
            def _():
                halo_copy(s, 1, up).wait_recv()

            halo = fields[s, near : near + DEEP, :].astype(F32)
            if start_near is None:
                start_near = jnp.concatenate([start, halo], axis=0)
            u = jnp.concatenate([now.astype(F32), halo], axis=0)
            now = (start_near - sweep(s, pick_ref[...], u, y_re, yi)).astype(BF16)
            fields[s + 1, 0:elems, :] = now[:elems]
            fields[s + 1, near : near + DEEP, :] = now[elems:]
            u = now[:elems].astype(F32)
            now = start - sweep(s + 1, pick_ref[:, 0:elems, :], u, y_re[:elems], yi[:elems])
            now = now.astype(BF16)
        return now

    start = combine(dot(halves(forcing.astype(BF16)), inv_pad[...]))
    state = sweeps(0, start, pick_fwd, w_fwd, y_im, lambda: None)
    state_f = state.astype(F32)
    source = weight * state_f
    start = combine(dot(halves(source.astype(BF16)), inv_herm[...]))
    walls = []

    def beside():
        state_ref[...] = narrow(state_f, nb).astype(BF16)
        walls.extend(combine(dot(halves(state), liner_pad[...])))

    adjoint = sweeps(SWEEPS, start, pick_adj, w_adj, -y_im, beside)
    adjoint_f = adjoint.astype(F32)
    wall_re, wall_im = walls
    a, b = adjoint_f[:, :HALF], adjoint_f[:, HALF:]
    term_re = -jnp.sum(a * wall_re + b * wall_im, axis=1, keepdims=True) / 16.0
    term_im = -jnp.sum(b * wall_re - a * wall_im, axis=1, keepdims=True) / 16.0

    def grad_part(p):
        pick = face_pick(p)
        re = jnp.sum(jnp.where(pick, term_re, 0.0), axis=0, keepdims=True)
        im = jnp.sum(jnp.where(pick, term_im, 0.0), axis=0, keepdims=True)
        return jnp.concatenate([re, im, jnp.zeros((6, 128), F32)], axis=0)

    @pl.loop(1, n)
    def _(k):
        p = peer(k)
        grad_send[p] = grad_part(p)
        grad_copy(p, me).start()

    def take_grad(k, total):
        p = peer(n - k)
        grad_copy(p, p).wait_recv()
        return total + grad_recv[p]

    adjoint_ref[...] = narrow(adjoint_f, nb).astype(BF16)
    total = lax.fori_loop(1, n, take_grad, grad_part(me))
    grad_ref[...] = total[0:2, 0:lin]

    @pl.loop(1, n)
    def _(k):
        p = peer(k)
        src_copy(p, me).wait_send()
        adm_copy(p, me).wait_send()
        grad_copy(p, me).wait_send()

    @pl.when(has_up)
    def _():
        off_copy(0, up).wait_send()
        for s in range(0, 2 * SWEEPS, 2):
            halo_copy(s, 0, up).wait_send()

    @pl.when(has_down)
    def _():
        off_copy(1, down).wait_send()
        for s in range(0, 2 * SWEEPS, 2):
            halo_copy(s, 1, down).wait_send()


def finish(state_in, adjoint_in, grad_in, state_out, adjoint_out, grad_out, sems):
    pairs = ((state_in, state_out), (adjoint_in, adjoint_out), (grad_in, grad_out))
    moves = [pltpu.make_async_copy(a, b, sems.at[i]) for i, (a, b) in enumerate(pairs)]
    for move in moves:
        move.start()
    for move in moves:
        move.wait()


def solution(mesh):
    n = mesh.shape["mesh"]

    def local(
        src_rows,
        src_owner,
        src_slot,
        neighbour_offset,
        liner_face,
        admittance,
        observe_weight,
        coupling,
        block_inv,
        liner_op,
    ):
        rows, width = src_rows.shape
        elems = liner_face.shape[0]
        lin = admittance.shape[1]
        vmem = pl.BlockSpec(memory_space=pltpu.VMEM)
        dma = pltpu.SemaphoreType.DMA
        parts = tuple(
            pl.pallas_call(
                functools.partial(kernel, n),
                out_shape=(
                    pltpu.VMEM((elems, width), BF16),
                    pltpu.VMEM((elems, width), BF16),
                    pltpu.VMEM((2, lin), F32),
                ),
                in_specs=[vmem] * 7 + [pl.BlockSpec(memory_space=pltpu.HBM)] * 3,
                out_specs=(vmem,) * 3,
                scratch_shapes=[
                    pltpu.VMEM((n, elems, width), BF16),
                    pltpu.VMEM((n, elems, width), BF16),
                    pltpu.VMEM((8, 128), F32),
                    pltpu.VMEM((n, 8, 128), F32),
                    pltpu.VMEM((8, 128), F32),
                    pltpu.VMEM((2, 8, 128), F32),
                    pltpu.VMEM((n, 8, 128), F32),
                    pltpu.VMEM((n, 8, 128), F32),
                    pltpu.VMEM((2 * SWEEPS, 128, FULL), BF16),
                    pltpu.VMEM(((FACES + 1) * HALF, FULL), BF16),
                    pltpu.VMEM(((FACES + 1) * HALF, FULL), BF16),
                    pltpu.VMEM((HALF, FULL), BF16),
                    pltpu.VMEM((HALF, FULL), BF16),
                    pltpu.VMEM((HALF, FULL), BF16),
                    pltpu.VMEM((HALF, FULL), BF16),
                    pltpu.VMEM((FACES, elems + DEEP, 128), BF16),
                    pltpu.VMEM((FACES, elems + DEEP, 128), BF16),
                    dma((2, n)),
                    dma((2, n)),
                    dma((2, 2)),
                    dma((2, n)),
                    dma((2, SWEEPS, 2)),
                    pltpu.VMEM(coupling.shape, BF16),
                    pltpu.VMEM(block_inv.shape, BF16),
                    pltpu.VMEM(liner_op.shape, BF16),
                    dma((3,)),
                ],
                compiler_params=pltpu.CompilerParams(
                    collective_id=0, has_side_effects=True, vmem_limit_bytes=2**26 - 2**21
                ),
            )(*(pltpu.with_memory_space_constraint(x, pltpu.HBM) for x in (
                src_owner.reshape(1, rows),
                src_slot.reshape(1, rows),
                neighbour_offset.T,
                liner_face.reshape(1, elems),
                admittance,
                observe_weight.reshape(1, elems),
                src_rows,
                coupling,
                block_inv,
                liner_op,
            )))
        )
        hbm = pl.BlockSpec(memory_space=pl.ANY)
        return tuple(
            pl.pallas_call(
                finish,
                out_shape=tuple(jax.ShapeDtypeStruct(x.shape, x.dtype) for x in parts),
                in_specs=[hbm] * 3,
                out_specs=(hbm,) * 3,
                scratch_shapes=[pltpu.SemaphoreType.DMA((3,))],
                compiler_params=pltpu.CompilerParams(vmem_limit_bytes=2**20),
            )(*parts)
        )

    placed = (
        P(("mode", "mesh"), None),
        P(("mode", "mesh"), None),
        P(("mode", "mesh")),
        P(("mode", "mesh"), None),
        P(("mode", "mesh")),
        P("mode", "mesh"),
        P(("mode", "mesh")),
        P("mode", None, None),
        P("mode", None),
        P("mode", None),
    )
    return jax.shard_map(
        local,
        mesh=mesh,
        in_specs=placed,
        out_specs=(P(("mode", "mesh"), None), P(("mode", "mesh"), None), P("mode", "mesh")),
        check_vma=False,
    )
```

```python
import functools

import jax
import jax.numpy as jnp
from jax import lax
from jax.experimental import pallas as pl
from jax.experimental.pallas import tpu as pltpu
from jax.sharding import PartitionSpec as P

SWEEPS = 4
RIM = 16
FACES = 6
QUAD = 4
LANES = 128
MESH = pl.DeviceIdType.MESH
F32 = jnp.float32
BF16 = jnp.bfloat16


def iota(shape, dim):
    return lax.broadcasted_iota(jnp.int32, shape, dim)


def dot(a, b):
    return jnp.dot(a, b, preferred_element_type=F32)


def swap(x):
    return pltpu.roll(x, x.shape[1] // 2, 1)


def first(x):
    return iota(x.shape, 1) < x.shape[1] // 2


def times_i(x):
    turned = swap(x)
    return jnp.where(first(x), -turned, turned)


def full(x):
    x = x.astype(F32)
    return jnp.concatenate([x, times_i(x)], axis=0)


def kernel(
    n,
    owner_hbm,
    slot_hbm,
    off_hbm,
    face_hbm,
    adm_hbm,
    weight_hbm,
    src_hbm,
    coupling_hbm,
    inv_hbm,
    liner_hbm,
    state_ref,
    adjoint_ref,
    grad_ref,
    owner_ref,
    slot_ref,
    off_ref,
    face_ref,
    adm_ref,
    weight_ref,
    src_ref,
    coupling_ref,
    inv_ref,
    liner_ref,
    load_sems,
    far_send,
    near_send,
    mid,
    summed,
    near_recv,
    far_recv,
    mid_sems,
    near_sems,
    far_sems,
    adm_send,
    adm_recv,
    adm_sems,
    off_send,
    off_halo,
    off_sems,
    grad_send,
    grad_recv,
    grad_sems,
    ext,
    halo_sems,
    start_ref,
    field_re,
    field_im,
    wall_re,
    wall_im,
    inv_full,
    inv_herm,
    liner_full,
    w_fwd,
    w_adj,
    pick_fwd_ends,
    pick_adj_ends,
    pick_fwd_mid,
    pick_adj_mid,
):
    me = lax.axis_index("mesh")
    elems = off_ref.shape[1]
    nb, width = inv_ref.shape
    lin = adm_ref.shape[1]
    rows = src_ref.shape[0]
    faces = adm_send.shape[1]
    wide = wall_re.shape[1]
    quads = n // QUAD
    pieces = summed.shape[1]
    piece = elems // pieces
    own = pl.ds(elems, elems)

    up, down = jnp.minimum(me + 1, n - 1), jnp.maximum(me - 1, 0)
    has_up, has_down = me < n - 1, me > 0

    barrier = pltpu.get_barrier_semaphore()
    for k in range(1, n):
        pl.semaphore_signal(
            barrier, inc=1, device_id={"mesh": lax.rem(me + k, n)}, device_id_type=MESH
        )

    loads = [
        pltpu.make_async_copy(hbm, here, load_sems.at[i])
        for i, (hbm, here) in enumerate(
            (
                (owner_hbm, owner_ref),
                (slot_hbm, slot_ref),
                (src_hbm, src_ref),
                (off_hbm, off_ref),
                (face_hbm, face_ref),
                (weight_hbm, weight_ref),
                (adm_hbm, adm_ref),
                (inv_hbm, inv_ref),
                (coupling_hbm, coupling_ref),
                (liner_hbm, liner_ref),
            )
        )
    ]
    for load in loads:
        load.start()

    def to(src, dst, sems, at, p):
        return pltpu.make_async_remote_copy(
            src_ref=src,
            dst_ref=dst,
            send_sem=sems.at[(0, *at)],
            recv_sem=sems.at[(1, *at)],
            device_id={"mesh": p},
            device_id_type=MESH,
        )

    q, r = me // QUAD, lax.rem(me, QUAD)
    high, low = r // 2, lax.rem(r, 2)
    near = [2 * high + 1 - low, 2 * (1 - high) + low, 2 * (1 - high) + 1 - low]

    def quad_at(t):
        return lax.rem(q + t, quads)

    def mid_copy(j, t, h):
        part = pl.ds(h * piece, piece)
        return to(
            far_send.at[j, t - 1, part],
            mid.at[j, t - 1, part],
            mid_sems,
            (j, t - 1, h),
            q * QUAD + near[j],
        )

    def near_copy(j):
        return to(near_send.at[j], near_recv.at[j], near_sems, (j,), q * QUAD + near[j])

    def far_copy(t, h):
        return to(
            summed.at[t - 1, h],
            far_recv.at[t - 1, pl.ds(h * piece, piece)],
            far_sems,
            (t - 1, h),
            quad_at(t) * QUAD + r,
        )

    def adm_copy(k):
        return to(adm_send, adm_recv.at[k - 1], adm_sems, (k - 1,), lax.rem(me + k, n))

    def grad_copy(k):
        return to(grad_send, grad_recv.at[k - 1], grad_sems, (k - 1,), lax.rem(me + k, n))

    def off_copy(side):
        return to(off_send, off_halo.at[side], off_sems, (side,), up if side == 0 else down)

    def halo_copy(solve, side):
        there = pl.ds(0 if side == 0 else 2 * elems, elems)
        return to(
            ext.at[solve, own],
            ext.at[solve, there],
            halo_sems,
            (solve, side),
            up if side == 0 else down,
        )

    def each_side(copy, what, incoming):
        @pl.when(has_down if incoming else has_up)
        def _():
            getattr(copy(0), what)()

        @pl.when(has_up if incoming else has_down)
        def _():
            getattr(copy(1), what)()

    @pl.when(jnp.logical_not(has_down))
    def _():
        off_halo[0] = jnp.zeros((8, LANES), F32)
        for solve in range(2):
            ext[solve, 0:elems] = jnp.zeros((elems, width), BF16)

    @pl.when(jnp.logical_not(has_up))
    def _():
        off_halo[1] = jnp.zeros((8, LANES), F32)
        for solve in range(2):
            ext[solve, 2 * elems : 3 * elems] = jnp.zeros((elems, width), BF16)

    for load in loads[:3]:
        load.wait()
    target = owner_ref[...] * elems + slot_ref[...]

    def partial_sum(p):
        pick = (iota((elems, rows), 0) + p * elems) == target
        return dot(pick.astype(F32).astype(BF16), src_ref[...])

    for t in range(1, quads):
        for j in range(QUAD - 1):
            far_send[j, t - 1] = partial_sum(quad_at(t) * QUAD + near[j]).astype(BF16)

    for load in loads[3:7]:
        load.wait()
    off_send[...] = jnp.zeros_like(off_send)
    off_send[0:FACES, 0:elems] = off_ref[...].astype(F32)
    off_send[FACES : FACES + 1, 0:elems] = face_ref[...].astype(F32)
    off_send[FACES + 1 : FACES + 2, 0:elems] = weight_ref[...]
    adm_send[...] = jnp.zeros_like(adm_send)
    adm_send[0:2, 0:lin] = adm_ref[...]
    place = me * lin
    turned = pltpu.roll(adm_send[:, :LANES], lax.rem(place, LANES), 1)
    lane_f = iota((8, faces), 1)
    mine_f = jnp.logical_and(lane_f >= place, lane_f < place + lin)
    adm_send[...] = jnp.where(
        mine_f, jnp.concatenate([turned] * (faces // LANES), axis=1), 0.0
    )

    pl.semaphore_wait(barrier, n - 1)
    for h in range(pieces):
        for t in range(1, quads):
            for j in (2, 0, 1):
                mid_copy(j, t, h).start()
    each_side(off_copy, "start", False)
    for k in range(1, n):
        adm_copy(k).start()
    for j in (2, 0, 1):
        near_send[j] = partial_sum(q * QUAD + near[j]).astype(BF16)
        near_copy(j).start()

    loads[7].wait()
    inv_wide = full(inv_ref[...])
    inv_full[...] = inv_wide.astype(BF16)
    loads[8].wait()

    @pl.loop(0, FACES)
    def _(f):
        at = pl.ds(pl.multiple_of(f * nb, nb), nb)
        w_fwd[at, :] = dot(coupling_ref[f], inv_full[...]).astype(BF16)

    loads[9].wait()
    w_fwd[FACES * nb : (FACES + 1) * nb, :] = dot(liner_ref[...], inv_full[...]).astype(BF16)
    depth = w_fwd.shape[0]
    over = depth - (FACES + 1) * nb
    w_fwd[depth - over :, :] = jnp.zeros((over, width), BF16)
    w_adj[depth - over :, :] = jnp.zeros((over, width), BF16)

    for h in range(pieces):
        for t in range(1, quads):
            total = partial_sum(quad_at(t) * QUAD + r)[h * piece : (h + 1) * piece]
            for j in (2, 0, 1):
                mid_copy(j, t, h).wait_recv()
                total = total + mid[j, t - 1, h * piece : (h + 1) * piece].astype(F32)
            summed[t - 1, h] = total.astype(BF16)
            far_copy(t, h).start()

    def fold_adjoint(f, matrix):
        turned = dot(inv_ref[...], full(matrix).astype(BF16))
        turned = jnp.concatenate([turned, jnp.zeros((wide - nb, width), F32)], axis=0).T
        rest = jnp.zeros((nb, width - wide), F32)
        re = jnp.concatenate([turned[:nb], rest], axis=1)
        im = jnp.concatenate([turned[nb:], rest], axis=1)
        at = pl.ds(f * nb if isinstance(f, int) else pl.multiple_of(f * nb, nb), nb)
        w_adj[at, :] = (re - swap(im)).astype(BF16)

    inv_herm[...] = inv_wide.T.astype(BF16)
    liner_full[...] = full(liner_ref[...]).astype(BF16)
    fold_adjoint(FACES, liner_ref[...])

    each_side(off_copy, "wait_recv", True)
    lane = iota((8, LANES), 1)
    offs = jnp.concatenate(
        [
            jnp.where(lane < elems, off_halo[0], pltpu.roll(off_send[...], elems, 1)),
            jnp.where(lane < elems, off_halo[1], 0.0),
        ],
        axis=1,
    )
    offs_col = jnp.concatenate([offs, jnp.zeros((LANES - 8, 2 * LANES), F32)], axis=0).T

    def picks(out_lo, count, in_lo):
        place = iota((count, LANES), 0) + (out_lo - in_lo) - iota((count, LANES), 1)
        place = place.astype(F32)
        cols = offs_col[out_lo : out_lo + count]
        here = offs if in_lo == 0 else pltpu.roll(offs, 2 * LANES - in_lo, 1)
        here = here[:, :LANES]

        def hot(x):
            return jnp.where(x, 1.0, 0.0).astype(BF16)

        fwd = [hot(place + cols[:, f : f + 1] == 0.0) for f in range(FACES)]
        adj = [hot(place == here[f : f + 1, :]) for f in range(FACES)]
        return fwd, adj

    half = (3 * elems - 2 * RIM) // 2
    for side in range(2):
        fwd, adj = picks(RIM + side * half, half, side * elems)
        for f in range(FACES):
            at = pl.ds((f % 2) * LANES, LANES)
            pick_fwd_ends[side, f // 2, :, at] = fwd[f]
            pick_adj_ends[side, f // 2, :, at] = adj[f]
    mid_rows = pick_fwd_mid.shape[1]
    mid_lo = elems - (mid_rows - elems) // 2
    fwd, adj = picks(mid_lo, mid_rows, elems // 2)
    for f in range(FACES):
        at = pl.ds((f % 2) * LANES, LANES)
        pick_fwd_mid[f // 2, :, at] = fwd[f]
        pick_adj_mid[f // 2, :, at] = adj[f]

    table = adm_send[...]
    for k in range(1, n):
        adm_copy(k).wait_recv()
        table = table + adm_recv[k - 1]
    face_all = offs_col[: 3 * elems, FACES : FACES + 1]
    weight = offs_col[elems : 2 * elems, FACES + 1 : FACES + 2]
    has_face = face_all == iota((3 * elems, faces), 1).astype(F32)
    y_re = jnp.sum(jnp.where(has_face, table[0:1], 0.0), axis=1, keepdims=True)
    y_im = jnp.sum(jnp.where(has_face, table[1:2], 0.0), axis=1, keepdims=True)
    own_face = offs_col[elems : 2 * elems, FACES : FACES + 1]
    own_face = own_face == iota((elems, faces), 1).astype(F32)

    def put(lo, value, yi):
        count = value.shape[0]
        value = value.astype(BF16).astype(F32)
        turned = swap(value)
        is_re = first(value)
        at = pl.ds(lo, count)
        field_re[0, at] = jnp.where(is_re, value, 0.0).astype(BF16)
        field_re[1, at] = jnp.where(is_re, 0.0, turned).astype(BF16)
        field_im[0, at] = jnp.where(is_re, turned, 0.0).astype(BF16)
        field_im[1, at] = jnp.where(is_re, 0.0, value).astype(BF16)
        a, b = y_re[lo : lo + count], yi[lo : lo + count]
        re, im = value[:, :wide], turned[:, :wide]
        wall_re[at] = (a * re - b * im).astype(BF16)
        wall_im[at] = (a * im + b * re).astype(BF16)

    def sweep(s, ends, middle, w_ref):
        lo = RIM * s
        hi = 3 * elems - lo
        if hi - lo > mid_rows:
            centre = 3 * elems // 2
            blocks = [(ends.at[0, :, lo - RIM : half], 0), (ends.at[1, :, 0 : hi - centre], elems)]
        else:
            blocks = [(middle.at[:, lo - mid_lo : hi - mid_lo], elems // 2)]

        def met(field):
            parts = [[] for _ in range(FACES // 2)]
            for pick, in_lo in blocks:
                count = pick.shape[1]
                got = dot(
                    pick[...].reshape(FACES // 2 * count, 2 * LANES),
                    field[:, in_lo : in_lo + LANES].reshape(2 * LANES, width),
                ).astype(BF16)
                for i, part in enumerate(parts):
                    part.append(got[i * count : (i + 1) * count])
            return [jnp.concatenate(part, axis=0) for part in parts]

        left = jnp.concatenate(
            [
                jnp.concatenate(met(field_re) + [wall_re[lo:hi]], axis=1),
                jnp.concatenate(met(field_im) + [wall_im[lo:hi]], axis=1),
            ],
            axis=0,
        )
        prod = dot(left, w_ref[...])
        count = hi - lo
        return start_ref[lo:hi] - (prod[:count] + times_i(prod[count:]))

    def solve(which, start, ends, middle, w_ref, yi, beside):
        ext[which, own] = start.astype(BF16)
        each_side(lambda side: halo_copy(which, side), "start", False)
        start_ref[own] = start
        put(elems, start, yi)
        beside()
        each_side(lambda side: halo_copy(which, side), "wait_recv", True)
        for lo in (0, 2 * elems):
            halo = ext[which, lo : lo + elems].astype(F32)
            start_ref[lo : lo + elems] = halo
            put(lo, halo, yi)
        for s in range(1, SWEEPS + 1):
            now = sweep(s, ends, middle, w_ref)
            if s < SWEEPS:
                put(RIM * s, now, yi)
        return now.astype(BF16)

    forcing = partial_sum(me)
    for j in (0, 1, 2):
        near_copy(j).wait_recv()
        forcing = forcing + near_recv[j].astype(F32)
    for t in range(1, quads):
        for h in range(pieces):
            far_copy(t, h).wait_recv()
        forcing = forcing + far_recv[t - 1].astype(F32)

    def fold_rest():
        @pl.loop(0, FACES)
        def _(f):
            fold_adjoint(f, coupling_ref[f])

    state = solve(
        0,
        dot(forcing.astype(BF16), inv_full[...]),
        pick_fwd_ends,
        pick_fwd_mid,
        w_fwd,
        y_im,
        fold_rest,
    )
    source = weight * state.astype(F32)
    walls = []

    def beside():
        state_ref[...] = state
        walls.append(dot(state, liner_full[...]))

    adjoint = solve(
        1,
        dot(source.astype(BF16), inv_herm[...]),
        pick_adj_ends,
        pick_adj_mid,
        w_adj,
        -y_im,
        beside,
    )
    adjoint_f = adjoint.astype(F32)
    wall = walls[0]
    term_re = jnp.sum(adjoint_f * wall, axis=1, keepdims=True) / -16.0
    term_im = jnp.sum(adjoint_f * times_i(wall), axis=1, keepdims=True) / -16.0
    grad_re = jnp.sum(jnp.where(own_face, term_re, 0.0), axis=0, keepdims=True)
    grad_im = jnp.sum(jnp.where(own_face, term_im, 0.0), axis=0, keepdims=True)
    total = jnp.concatenate([grad_re, grad_im, jnp.zeros((6, faces), F32)], axis=0)
    grad_send[...] = total
    for k in range(1, n):
        grad_copy(k).start()
    adjoint_ref[...] = adjoint
    for k in range(1, n):
        grad_copy(k).wait_recv()
        total = total + grad_recv[k - 1]
    total = jnp.where(mine_f, total, 0.0)
    parts = [total[:, i : i + LANES] for i in range(0, faces, LANES)]
    turned = pltpu.roll(sum(parts[1:], parts[0]), LANES - lax.rem(place, LANES), 1)
    grad_ref[...] = turned[0:2, 0:lin]

    for t in range(1, quads):
        for h in range(pieces):
            for j in range(QUAD - 1):
                mid_copy(j, t, h).wait_send()
            far_copy(t, h).wait_send()
    for j in range(QUAD - 1):
        near_copy(j).wait_send()
    for k in range(1, n):
        adm_copy(k).wait_send()
        grad_copy(k).wait_send()
    each_side(off_copy, "wait_send", False)
    for which in range(2):
        each_side(lambda side: halo_copy(which, side), "wait_send", False)


def finish(state_in, adjoint_in, grad_in, state_out, adjoint_out, grad_out, sems):
    pairs = ((state_in, state_out), (adjoint_in, adjoint_out), (grad_in, grad_out))
    moves = [pltpu.make_async_copy(a, b, sems.at[i]) for i, (a, b) in enumerate(pairs)]
    for move in moves:
        move.start()
    for move in moves:
        move.wait()


def solution(mesh):
    n = mesh.shape["mesh"]

    def local(
        src_rows,
        src_owner,
        src_slot,
        neighbour_offset,
        liner_face,
        admittance,
        observe_weight,
        coupling,
        block_inv,
        liner_op,
    ):
        rows, width = src_rows.shape
        nb = width // 2
        elems = liner_face.shape[0]
        lin = admittance.shape[1]
        faces = n * lin
        quads = n // QUAD
        pieces = 2
        wide = -(-nb // LANES) * LANES
        half = (3 * elems - 2 * RIM) // 2
        others = max(quads - 1, 1)
        vmem, dma = pltpu.VMEM, pltpu.SemaphoreType.DMA
        args = (
            src_owner.reshape(1, rows),
            src_slot.reshape(1, rows),
            neighbour_offset.T,
            liner_face.reshape(1, elems),
            admittance,
            observe_weight.reshape(1, elems),
            src_rows,
            coupling,
            block_inv,
            liner_op,
        )
        parts = pl.pallas_call(
            functools.partial(kernel, n),
            out_shape=(
                vmem((elems, width), BF16),
                vmem((elems, width), BF16),
                vmem((2, lin), F32),
            ),
            in_specs=[pl.BlockSpec(memory_space=pltpu.HBM)] * len(args),
            out_specs=(pl.BlockSpec(memory_space=pltpu.VMEM),) * 3,
            scratch_shapes=[vmem(x.shape, x.dtype) for x in args]
            + [
                dma((len(args),)),
                vmem((QUAD - 1, others, elems, width), BF16),
                vmem((QUAD - 1, elems, width), BF16),
                vmem((QUAD - 1, others, elems, width), BF16),
                vmem((others, pieces, elems // pieces, width), BF16),
                vmem((QUAD - 1, elems, width), BF16),
                vmem((others, elems, width), BF16),
                dma((2, QUAD - 1, others, pieces)),
                dma((2, QUAD - 1)),
                dma((2, others, pieces)),
                vmem((8, faces), F32),
                vmem((n - 1, 8, faces), F32),
                dma((2, n - 1)),
                vmem((8, LANES), F32),
                vmem((2, 8, LANES), F32),
                dma((2, 2)),
                vmem((8, faces), F32),
                vmem((n - 1, 8, faces), F32),
                dma((2, n - 1)),
                vmem((2, 3 * elems, width), BF16),
                dma((2, 2, 2)),
                vmem((3 * elems, width), F32),
                vmem((2, 3 * elems, width), BF16),
                vmem((2, 3 * elems, width), BF16),
                vmem((3 * elems, wide), BF16),
                vmem((3 * elems, wide), BF16),
                vmem((width, width), BF16),
                vmem((width, width), BF16),
                vmem((width, width), BF16),
                vmem((FACES * nb + wide, width), BF16),
                vmem((FACES * nb + wide, width), BF16),
                vmem((2, FACES // 2, half, 2 * LANES), BF16),
                vmem((2, FACES // 2, half, 2 * LANES), BF16),
                vmem((FACES // 2, LANES - 2 * RIM, 2 * LANES), BF16),
                vmem((FACES // 2, LANES - 2 * RIM, 2 * LANES), BF16),
            ],
            compiler_params=pltpu.CompilerParams(
                collective_id=0, has_side_effects=True, vmem_limit_bytes=2**26 - 2**21
            ),
        )(*(pltpu.with_memory_space_constraint(x, pltpu.HBM) for x in args))
        anywhere = pl.BlockSpec(memory_space=pl.ANY)
        return tuple(
            pl.pallas_call(
                finish,
                out_shape=tuple(jax.ShapeDtypeStruct(x.shape, x.dtype) for x in parts),
                in_specs=[anywhere] * 3,
                out_specs=(anywhere,) * 3,
                scratch_shapes=[dma((3,))],
                compiler_params=pltpu.CompilerParams(vmem_limit_bytes=2**20),
            )(*parts)
        )

    placed = (
        P(("mode", "mesh"), None),
        P(("mode", "mesh"), None),
        P(("mode", "mesh")),
        P(("mode", "mesh"), None),
        P(("mode", "mesh")),
        P("mode", "mesh"),
        P(("mode", "mesh")),
        P("mode", None, None),
        P("mode", None),
        P("mode", None),
    )
    return jax.shard_map(
        local,
        mesh=mesh,
        in_specs=placed,
        out_specs=(P(("mode", "mesh"), None), P(("mode", "mesh"), None), P("mode", "mesh")),
        check_vma=False,
    )
```

```python
import functools

import jax
import jax.numpy as jnp
from jax import lax
from jax.experimental import pallas as pl
from jax.experimental.pallas import tpu as pltpu
from jax.sharding import PartitionSpec as P

SWEEPS = 4
RIM = 16
FACES = 6
QUAD = 4
LANES = 128
MESH = pl.DeviceIdType.MESH
F32 = jnp.float32
BF16 = jnp.bfloat16


def iota(shape, dim):
    return lax.broadcasted_iota(jnp.int32, shape, dim)


def dot(a, b):
    return jnp.dot(a, b, preferred_element_type=F32)


def swap(x):
    return pltpu.roll(x, x.shape[1] // 2, 1)


def first(x):
    return iota(x.shape, 1) < x.shape[1] // 2


def times_i(x):
    turned = swap(x)
    return jnp.where(first(x), -turned, turned)


def full(x):
    x = x.astype(F32)
    return jnp.concatenate([x, times_i(x)], axis=0)


def kernel(
    n,
    owner_hbm,
    slot_hbm,
    off_hbm,
    face_hbm,
    adm_hbm,
    weight_hbm,
    src_hbm,
    coupling_hbm,
    inv_hbm,
    liner_hbm,
    state_ref,
    adjoint_ref,
    grad_ref,
    owner_ref,
    slot_ref,
    off_ref,
    face_ref,
    adm_ref,
    weight_ref,
    src_ref,
    coupling_ref,
    inv_ref,
    liner_ref,
    load_sems,
    far_send,
    near_send,
    mid,
    summed,
    near_recv,
    far_recv,
    mid_sems,
    near_sems,
    far_sems,
    adm_send,
    adm_recv,
    adm_sems,
    off_send,
    off_halo,
    off_sems,
    grad_send,
    grad_recv,
    grad_sems,
    ext,
    halo_sems,
    start_ref,
    field_re,
    field_im,
    wall_re,
    wall_im,
    inv_full,
    inv_herm,
    liner_full,
    w_fwd,
    w_adj,
    pick_fwd_ends,
    pick_adj_ends,
    pick_fwd_mid,
    pick_adj_mid,
):
    me = lax.axis_index("mesh")
    elems = off_ref.shape[1]
    nb, width = inv_ref.shape
    lin = adm_ref.shape[1]
    rows = src_ref.shape[0]
    faces = adm_send.shape[1]
    wide = wall_re.shape[2]
    quads = n // QUAD
    pieces = summed.shape[1]
    piece = elems // pieces
    own = pl.ds(elems, elems)

    up, down = jnp.minimum(me + 1, n - 1), jnp.maximum(me - 1, 0)
    has_up, has_down = me < n - 1, me > 0

    barrier = pltpu.get_barrier_semaphore()
    for k in range(1, n):
        pl.semaphore_signal(
            barrier, inc=1, device_id={"mesh": lax.rem(me + k, n)}, device_id_type=MESH
        )

    loads = [
        pltpu.make_async_copy(hbm, here, load_sems.at[i])
        for i, (hbm, here) in enumerate(
            (
                (owner_hbm, owner_ref),
                (slot_hbm, slot_ref),
                (src_hbm, src_ref),
                (off_hbm, off_ref),
                (face_hbm, face_ref),
                (weight_hbm, weight_ref),
                (adm_hbm, adm_ref),
                (inv_hbm, inv_ref),
                (coupling_hbm, coupling_ref),
                (liner_hbm, liner_ref),
            )
        )
    ]
    for load in loads:
        load.start()

    def to(src, dst, sems, at, p):
        return pltpu.make_async_remote_copy(
            src_ref=src,
            dst_ref=dst,
            send_sem=sems.at[(0, *at)],
            recv_sem=sems.at[(1, *at)],
            device_id={"mesh": p},
            device_id_type=MESH,
        )

    q, r = me // QUAD, lax.rem(me, QUAD)
    high, low = r // 2, lax.rem(r, 2)
    near = [2 * high + 1 - low, 2 * (1 - high) + low, 2 * (1 - high) + 1 - low]

    def quad_at(t):
        return lax.rem(q + t, quads)

    def mid_copy(j, t, h):
        part = pl.ds(h * piece, piece)
        return to(
            far_send.at[j, t - 1, part],
            mid.at[j, t - 1, part],
            mid_sems,
            (j, t - 1, h),
            q * QUAD + near[j],
        )

    def near_copy(j):
        return to(near_send.at[j], near_recv.at[j], near_sems, (j,), q * QUAD + near[j])

    def far_copy(t, h):
        return to(
            summed.at[t - 1, h],
            far_recv.at[t - 1, pl.ds(h * piece, piece)],
            far_sems,
            (t - 1, h),
            quad_at(t) * QUAD + r,
        )

    def adm_copy(k):
        return to(adm_send, adm_recv.at[k - 1], adm_sems, (k - 1,), lax.rem(me + k, n))

    def grad_copy(k):
        return to(grad_send, grad_recv.at[k - 1], grad_sems, (k - 1,), lax.rem(me + k, n))

    def off_copy(side):
        return to(off_send, off_halo.at[side], off_sems, (side,), up if side == 0 else down)

    def halo_copy(solve, reach, side):
        mine = elems + (elems // 2 if (side == 0) == (reach == 0) else 0)
        there = mine - elems if side == 0 else mine + elems
        return to(
            ext.at[solve, pl.ds(mine, elems // 2)],
            ext.at[solve, pl.ds(there, elems // 2)],
            halo_sems,
            (solve, reach, side),
            up if side == 0 else down,
        )

    def each_side(copy, what, incoming):
        @pl.when(has_down if incoming else has_up)
        def _():
            getattr(copy(0), what)()

        @pl.when(has_up if incoming else has_down)
        def _():
            getattr(copy(1), what)()

    @pl.when(jnp.logical_not(has_down))
    def _():
        off_halo[0] = jnp.zeros((8, LANES), F32)
        for solve in range(2):
            ext[solve, 0:elems] = jnp.zeros((elems, width), BF16)

    @pl.when(jnp.logical_not(has_up))
    def _():
        off_halo[1] = jnp.zeros((8, LANES), F32)
        for solve in range(2):
            ext[solve, 2 * elems : 3 * elems] = jnp.zeros((elems, width), BF16)

    field_re[...] = jnp.zeros_like(field_re)
    field_im[...] = jnp.zeros_like(field_im)
    for load in loads[:3]:
        load.wait()
    target = owner_ref[...] * elems + slot_ref[...]

    def partial_sum(p):
        pick = (iota((elems, rows), 0) + p * elems) == target
        return dot(pick.astype(F32).astype(BF16), src_ref[...])

    for t in range(1, quads):
        for j in range(QUAD - 1):
            far_send[j, t - 1] = partial_sum(quad_at(t) * QUAD + near[j]).astype(BF16)

    for load in loads[3:7]:
        load.wait()
    off_send[...] = jnp.zeros_like(off_send)
    off_send[0:FACES, 0:elems] = off_ref[...].astype(F32)
    off_send[FACES : FACES + 1, 0:elems] = face_ref[...].astype(F32)
    off_send[FACES + 1 : FACES + 2, 0:elems] = weight_ref[...]
    adm_send[...] = jnp.zeros_like(adm_send)
    adm_send[0:2, 0:lin] = adm_ref[...]
    place = me * lin
    turned = pltpu.roll(adm_send[:, :LANES], lax.rem(place, LANES), 1)
    lane_f = iota((8, faces), 1)
    mine_f = jnp.logical_and(lane_f >= place, lane_f < place + lin)
    adm_send[...] = jnp.where(
        mine_f, jnp.concatenate([turned] * (faces // LANES), axis=1), 0.0
    )

    pl.semaphore_wait(barrier, n - 1)
    for h in range(pieces):
        for t in range(1, quads):
            for j in (2, 0, 1):
                mid_copy(j, t, h).start()
    each_side(off_copy, "start", False)
    for k in range(1, n):
        adm_copy(k).start()
    for j in (2, 0, 1):
        near_send[j] = partial_sum(q * QUAD + near[j]).astype(BF16)
        near_copy(j).start()

    loads[7].wait()
    inv_wide = full(inv_ref[...])
    inv_full[...] = inv_wide.astype(BF16)
    loads[8].wait()

    @pl.loop(0, FACES)
    def _(f):
        at = pl.ds(pl.multiple_of(f * nb, nb), nb)
        w_fwd[at, :] = dot(coupling_ref[f], inv_full[...]).astype(BF16)

    loads[9].wait()
    w_fwd[FACES * nb : (FACES + 1) * nb, :] = dot(liner_ref[...], inv_full[...]).astype(BF16)
    depth = w_fwd.shape[0]
    over = depth - (FACES + 1) * nb
    w_fwd[depth - over :, :] = jnp.zeros((over, width), BF16)
    w_adj[depth - over :, :] = jnp.zeros((over, width), BF16)

    for h in range(pieces):
        for t in range(1, quads):
            total = partial_sum(quad_at(t) * QUAD + r)[h * piece : (h + 1) * piece]
            for j in (2, 0, 1):
                mid_copy(j, t, h).wait_recv()
                total = total + mid[j, t - 1, h * piece : (h + 1) * piece].astype(F32)
            summed[t - 1, h] = total.astype(BF16)
            far_copy(t, h).start()

    def fold_adjoint(f, matrix):
        turned = dot(inv_ref[...], full(matrix).astype(BF16))
        turned = jnp.concatenate([turned, jnp.zeros((wide - nb, width), F32)], axis=0).T
        rest = jnp.zeros((nb, width - wide), F32)
        re = jnp.concatenate([turned[:nb], rest], axis=1)
        im = jnp.concatenate([turned[nb:], rest], axis=1)
        at = pl.ds(f * nb if isinstance(f, int) else pl.multiple_of(f * nb, nb), nb)
        w_adj[at, :] = (re - swap(im)).astype(BF16)

    def fold_faces(begin, end):
        @pl.loop(begin, end)
        def _(f):
            fold_adjoint(f, coupling_ref[f])

    inv_herm[...] = inv_wide.T.astype(BF16)
    liner_full[...] = full(liner_ref[...]).astype(BF16)
    fold_adjoint(FACES, liner_ref[...])
    fold_faces(0, FACES // 3)

    each_side(off_copy, "wait_recv", True)
    lane = iota((8, LANES), 1)
    offs = jnp.concatenate(
        [
            jnp.where(lane < elems, off_halo[0], pltpu.roll(off_send[...], elems, 1)),
            jnp.where(lane < elems, off_halo[1], 0.0),
        ],
        axis=1,
    )
    offs_col = jnp.concatenate([offs, jnp.zeros((LANES - 8, 2 * LANES), F32)], axis=0).T

    def picks(out_lo, count, in_lo):
        place = iota((count, LANES), 0) + (out_lo - in_lo) - iota((count, LANES), 1)
        place = place.astype(F32)
        cols = offs_col[out_lo : out_lo + count]
        here = offs if in_lo == 0 else pltpu.roll(offs, 2 * LANES - in_lo, 1)
        here = here[:, :LANES]

        def hot(x):
            return jnp.where(x, 1.0, 0.0).astype(BF16)

        fwd = [hot(place + cols[:, f : f + 1] == 0.0) for f in range(FACES)]
        adj = [hot(place == here[f : f + 1, :]) for f in range(FACES)]
        return fwd, adj

    half = (3 * elems - 2 * RIM) // 2
    for side in range(2):
        fwd, adj = picks(RIM + side * half, half, side * elems)
        for f in range(FACES):
            at = pl.ds((f % 2) * LANES, LANES)
            pick_fwd_ends[side, f // 2, :, at] = fwd[f]
            pick_adj_ends[side, f // 2, :, at] = adj[f]
    mid_rows = pick_fwd_mid.shape[1]
    mid_lo = elems - (mid_rows - elems) // 2
    fwd, adj = picks(mid_lo, mid_rows, elems // 2)
    for f in range(FACES):
        at = pl.ds((f % 2) * LANES, LANES)
        pick_fwd_mid[f // 2, :, at] = fwd[f]
        pick_adj_mid[f // 2, :, at] = adj[f]

    table = adm_send[...]
    for k in range(1, n):
        adm_copy(k).wait_recv()
        table = table + adm_recv[k - 1]
    face_all = offs_col[: 3 * elems, FACES : FACES + 1]
    weight = offs_col[elems : 2 * elems, FACES + 1 : FACES + 2]
    has_face = face_all == iota((3 * elems, faces), 1).astype(F32)
    y_re = jnp.sum(jnp.where(has_face, table[0:1], 0.0), axis=1, keepdims=True)
    y_im = jnp.sum(jnp.where(has_face, table[1:2], 0.0), axis=1, keepdims=True)
    own_face = offs_col[elems : 2 * elems, FACES : FACES + 1]
    own_face = own_face == iota((elems, faces), 1).astype(F32)

    def put(s, lo, value, yi):
        count = value.shape[0]
        value = value.astype(BF16).astype(F32)
        turned = swap(value)
        is_re = first(value)
        at, b = pl.ds(lo, count), s % 2
        field_re[b, 0, at] = jnp.where(is_re, value, 0.0).astype(BF16)
        field_re[b, 1, at] = jnp.where(is_re, 0.0, turned).astype(BF16)
        field_im[b, 0, at] = jnp.where(is_re, turned, 0.0).astype(BF16)
        field_im[b, 1, at] = jnp.where(is_re, 0.0, value).astype(BF16)
        y_r, y_i = y_re[lo : lo + count], yi[lo : lo + count]
        re, im = value[:, :wide], turned[:, :wide]
        wall_re[b, at] = (y_r * re - y_i * im).astype(BF16)
        wall_im[b, at] = (y_r * im + y_i * re).astype(BF16)

    def rows_of(ref, spans):
        parts = [ref[lo:hi] for lo, hi in spans]
        return parts[0] if len(parts) == 1 else jnp.concatenate(parts, axis=0)

    def sweep(s, blocks, w_ref):
        b = (s - 1) % 2
        spans = [span for block in blocks for span in block[3]]

        def met(field):
            parts = [[] for _ in range(FACES // 2)]
            for pick, base, in_lo, wanted in blocks:
                picked = [pick[i, lo - base : hi - base] for i in range(FACES // 2) for lo, hi in wanted]
                got = dot(
                    jnp.concatenate(picked, axis=0),
                    field[b, :, in_lo : in_lo + LANES].reshape(2 * LANES, width),
                ).astype(BF16)
                count = got.shape[0] // (FACES // 2)
                for i, part in enumerate(parts):
                    part.append(got[i * count : (i + 1) * count])
            return [part[0] if len(part) == 1 else jnp.concatenate(part, axis=0) for part in parts]

        left = jnp.concatenate(
            [
                jnp.concatenate(met(field_re) + [rows_of(wall_re.at[b], spans)], axis=1),
                jnp.concatenate(met(field_im) + [rows_of(wall_im.at[b], spans)], axis=1),
            ],
            axis=0,
        )
        prod = dot(left, w_ref[...])
        count = prod.shape[0] // 2
        return rows_of(start_ref, spans) - (prod[:count] + times_i(prod[count:]))

    def solve(which, start, ends, middle, w_ref, yi, beside):
        ext[which, own] = start.astype(BF16)
        for reach in range(2):
            each_side(lambda side: halo_copy(which, reach, side), "start", False)
        start_ref[own] = start
        put(0, elems, start, yi)

        def lower(*spans):
            return (ends.at[0], RIM, 0, spans)

        def upper(*spans):
            return (ends.at[1], RIM + half, elems, spans)

        def centre(*spans):
            return (middle, mid_lo, elems // 2, spans)

        def first_sweep(*blocks):
            now = sweep(1, blocks, w_ref)
            at = 0
            for lo, hi in [span for block in blocks for span in block[3]]:
                put(1, lo, now[at : at + hi - lo], yi)
                at += hi - lo

        def arrive(reach):
            each_side(lambda side: halo_copy(which, reach, side), "wait_recv", True)
            for lo in (elems // 2 * (1 - reach), 2 * elems + elems // 2 * reach):
                halo = ext[which, lo : lo + elems // 2].astype(F32)
                start_ref[lo : lo + elems // 2] = halo
                put(0, lo, halo, yi)

        total = 3 * elems
        inner, near_lo, far_lo = elems + RIM, elems // 2 + RIM, RIM
        beside()
        first_sweep(centre((inner, total - inner)))
        arrive(0)
        first_sweep(centre((near_lo, inner), (total - inner, total - near_lo)))
        arrive(1)
        first_sweep(lower((far_lo, near_lo)), upper((total - near_lo, total - far_lo)))
        for s in range(2, SWEEPS + 1):
            lo, hi = RIM * s, total - RIM * s
            if hi - lo > mid_rows:
                blocks = (lower((lo, total // 2)), upper((total // 2, hi)))
            else:
                blocks = (centre((lo, hi)),)
            now = sweep(s, blocks, w_ref)
            if s < SWEEPS:
                put(s, lo, now, yi)
        return now.astype(BF16)

    forcing = partial_sum(me)
    for j in (0, 1, 2):
        near_copy(j).wait_recv()
        forcing = forcing + near_recv[j].astype(F32)
    for t in range(1, quads):
        for h in range(pieces):
            far_copy(t, h).wait_recv()
        forcing = forcing + far_recv[t - 1].astype(F32)

    state = solve(
        0,
        dot(forcing.astype(BF16), inv_full[...]),
        pick_fwd_ends,
        pick_fwd_mid,
        w_fwd,
        y_im,
        lambda: fold_faces(FACES // 3, 2 * FACES // 3),
    )
    source = weight * state.astype(F32)
    walls = []

    def beside():
        state_ref[...] = state
        walls.append(dot(state, liner_full[...]))
        fold_faces(2 * FACES // 3, FACES)

    adjoint = solve(
        1,
        dot(source.astype(BF16), inv_herm[...]),
        pick_adj_ends,
        pick_adj_mid,
        w_adj,
        -y_im,
        beside,
    )
    adjoint_f = adjoint.astype(F32)
    wall = walls[0]
    term_re = jnp.sum(adjoint_f * wall, axis=1, keepdims=True) / -16.0
    term_im = jnp.sum(adjoint_f * times_i(wall), axis=1, keepdims=True) / -16.0
    grad_re = jnp.sum(jnp.where(own_face, term_re, 0.0), axis=0, keepdims=True)
    grad_im = jnp.sum(jnp.where(own_face, term_im, 0.0), axis=0, keepdims=True)
    total = jnp.concatenate([grad_re, grad_im, jnp.zeros((6, faces), F32)], axis=0)
    grad_send[...] = total
    for k in range(1, n):
        grad_copy(k).start()
    adjoint_ref[...] = adjoint
    for k in range(1, n):
        grad_copy(k).wait_recv()
        total = total + grad_recv[k - 1]
    total = jnp.where(mine_f, total, 0.0)
    parts = [total[:, i : i + LANES] for i in range(0, faces, LANES)]
    turned = pltpu.roll(sum(parts[1:], parts[0]), LANES - lax.rem(place, LANES), 1)
    grad_ref[...] = turned[0:2, 0:lin]

    for t in range(1, quads):
        for h in range(pieces):
            for j in range(QUAD - 1):
                mid_copy(j, t, h).wait_send()
            far_copy(t, h).wait_send()
    for j in range(QUAD - 1):
        near_copy(j).wait_send()
    for k in range(1, n):
        adm_copy(k).wait_send()
        grad_copy(k).wait_send()
    each_side(off_copy, "wait_send", False)
    for which in range(2):
        for reach in range(2):
            each_side(lambda side: halo_copy(which, reach, side), "wait_send", False)


def finish(state_in, adjoint_in, grad_in, state_out, adjoint_out, grad_out, sems):
    pairs = ((state_in, state_out), (adjoint_in, adjoint_out), (grad_in, grad_out))
    moves = [pltpu.make_async_copy(a, b, sems.at[i]) for i, (a, b) in enumerate(pairs)]
    for move in moves:
        move.start()
    for move in moves:
        move.wait()


def solution(mesh):
    n = mesh.shape["mesh"]

    def local(
        src_rows,
        src_owner,
        src_slot,
        neighbour_offset,
        liner_face,
        admittance,
        observe_weight,
        coupling,
        block_inv,
        liner_op,
    ):
        rows, width = src_rows.shape
        nb = width // 2
        elems = liner_face.shape[0]
        lin = admittance.shape[1]
        faces = n * lin
        quads = n // QUAD
        pieces = 2
        wide = -(-nb // LANES) * LANES
        half = (3 * elems - 2 * RIM) // 2
        others = max(quads - 1, 1)
        vmem, dma = pltpu.VMEM, pltpu.SemaphoreType.DMA
        args = (
            src_owner.reshape(1, rows),
            src_slot.reshape(1, rows),
            neighbour_offset.T,
            liner_face.reshape(1, elems),
            admittance,
            observe_weight.reshape(1, elems),
            src_rows,
            coupling,
            block_inv,
            liner_op,
        )
        parts = pl.pallas_call(
            functools.partial(kernel, n),
            out_shape=(
                vmem((elems, width), BF16),
                vmem((elems, width), BF16),
                vmem((2, lin), F32),
            ),
            in_specs=[pl.BlockSpec(memory_space=pltpu.HBM)] * len(args),
            out_specs=(pl.BlockSpec(memory_space=pltpu.VMEM),) * 3,
            scratch_shapes=[vmem(x.shape, x.dtype) for x in args]
            + [
                dma((len(args),)),
                vmem((QUAD - 1, others, elems, width), BF16),
                vmem((QUAD - 1, elems, width), BF16),
                vmem((QUAD - 1, others, elems, width), BF16),
                vmem((others, pieces, elems // pieces, width), BF16),
                vmem((QUAD - 1, elems, width), BF16),
                vmem((others, elems, width), BF16),
                dma((2, QUAD - 1, others, pieces)),
                dma((2, QUAD - 1)),
                dma((2, others, pieces)),
                vmem((8, faces), F32),
                vmem((n - 1, 8, faces), F32),
                dma((2, n - 1)),
                vmem((8, LANES), F32),
                vmem((2, 8, LANES), F32),
                dma((2, 2)),
                vmem((8, faces), F32),
                vmem((n - 1, 8, faces), F32),
                dma((2, n - 1)),
                vmem((2, 3 * elems, width), BF16),
                dma((2, 2, 2, 2)),
                vmem((3 * elems, width), F32),
                vmem((2, 2, 3 * elems, width), BF16),
                vmem((2, 2, 3 * elems, width), BF16),
                vmem((2, 3 * elems, wide), BF16),
                vmem((2, 3 * elems, wide), BF16),
                vmem((width, width), BF16),
                vmem((width, width), BF16),
                vmem((width, width), BF16),
                vmem((FACES * nb + wide, width), BF16),
                vmem((FACES * nb + wide, width), BF16),
                vmem((2, FACES // 2, half, 2 * LANES), BF16),
                vmem((2, FACES // 2, half, 2 * LANES), BF16),
                vmem((FACES // 2, LANES - 2 * RIM, 2 * LANES), BF16),
                vmem((FACES // 2, LANES - 2 * RIM, 2 * LANES), BF16),
            ],
            compiler_params=pltpu.CompilerParams(
                collective_id=0, has_side_effects=True, vmem_limit_bytes=2**26 - 2**21
            ),
        )(*(pltpu.with_memory_space_constraint(x, pltpu.HBM) for x in args))
        anywhere = pl.BlockSpec(memory_space=pl.ANY)
        return tuple(
            pl.pallas_call(
                finish,
                out_shape=tuple(jax.ShapeDtypeStruct(x.shape, x.dtype) for x in parts),
                in_specs=[anywhere] * 3,
                out_specs=(anywhere,) * 3,
                scratch_shapes=[dma((3,))],
                compiler_params=pltpu.CompilerParams(vmem_limit_bytes=2**20),
            )(*parts)
        )

    placed = (
        P(("mode", "mesh"), None),
        P(("mode", "mesh"), None),
        P(("mode", "mesh")),
        P(("mode", "mesh"), None),
        P(("mode", "mesh")),
        P("mode", "mesh"),
        P(("mode", "mesh")),
        P("mode", None, None),
        P("mode", None),
        P("mode", None),
    )
    return jax.shard_map(
        local,
        mesh=mesh,
        in_specs=placed,
        out_specs=(P(("mode", "mesh"), None), P(("mode", "mesh"), None), P("mode", "mesh")),
        check_vma=False,
    )
```

```python
import functools

import jax
import jax.numpy as jnp
from jax import lax
from jax.experimental import pallas as pl
from jax.experimental.pallas import tpu as pltpu
from jax.sharding import PartitionSpec as P

SWEEPS = 4
RIM = 16
FACES = 6
QUAD = 4
LANES = 128
MESH = pl.DeviceIdType.MESH
F32 = jnp.float32
BF16 = jnp.bfloat16


def iota(shape, dim):
    return lax.broadcasted_iota(jnp.int32, shape, dim)


def dot(a, b):
    return jnp.dot(a, b, preferred_element_type=F32)


def swap(x):
    return pltpu.roll(x, x.shape[1] // 2, 1)


def first(x):
    return iota(x.shape, 1) < x.shape[1] // 2


def times_i(x):
    turned = swap(x)
    return jnp.where(first(x), -turned, turned)


def full(x):
    x = x.astype(F32)
    return jnp.concatenate([x, times_i(x)], axis=0)


def kernel(
    n,
    owner_hbm,
    slot_hbm,
    off_hbm,
    face_hbm,
    adm_hbm,
    weight_hbm,
    src_hbm,
    coupling_hbm,
    inv_hbm,
    liner_hbm,
    state_ref,
    adjoint_ref,
    grad_ref,
    owner_ref,
    slot_ref,
    off_ref,
    face_ref,
    adm_ref,
    weight_ref,
    src_ref,
    coupling_ref,
    inv_ref,
    liner_ref,
    load_sems,
    far_send,
    near_send,
    mid,
    summed,
    near_recv,
    far_recv,
    mid_sems,
    near_sems,
    far_sems,
    adm_send,
    adm_recv,
    adm_sems,
    off_send,
    off_halo,
    off_sems,
    grad_send,
    grad_recv,
    grad_sems,
    ext,
    halo_sems,
    start_ref,
    field_re,
    field_im,
    wall_re,
    wall_im,
    inv_full,
    inv_herm,
    liner_full,
    w_fwd,
    w_adj,
    pick_fwd_ends,
    pick_adj_ends,
    pick_fwd_mid,
    pick_adj_mid,
    admit_ref,
):
    me = lax.axis_index("mesh")
    elems = off_ref.shape[1]
    nb, width = inv_ref.shape
    lin = adm_ref.shape[1]
    rows = src_ref.shape[0]
    faces = adm_send.shape[1]
    wide = wall_re.shape[2]
    quads = n // QUAD
    pieces = summed.shape[1]
    piece = elems // pieces
    own = pl.ds(elems, elems)

    up, down = jnp.minimum(me + 1, n - 1), jnp.maximum(me - 1, 0)
    has_up, has_down = me < n - 1, me > 0

    barrier = pltpu.get_barrier_semaphore()
    for k in range(1, n):
        pl.semaphore_signal(
            barrier, inc=1, device_id={"mesh": lax.rem(me + k, n)}, device_id_type=MESH
        )

    loads = [
        pltpu.make_async_copy(hbm, here, load_sems.at[i])
        for i, (hbm, here) in enumerate(
            (
                (owner_hbm, owner_ref),
                (slot_hbm, slot_ref),
                (src_hbm, src_ref),
                (off_hbm, off_ref),
                (face_hbm, face_ref),
                (weight_hbm, weight_ref),
                (adm_hbm, adm_ref),
                (inv_hbm, inv_ref),
                (coupling_hbm, coupling_ref),
                (liner_hbm, liner_ref),
            )
        )
    ]
    for load in loads:
        load.start()

    def to(src, dst, sems, at, p):
        return pltpu.make_async_remote_copy(
            src_ref=src,
            dst_ref=dst,
            send_sem=sems.at[(0, *at)],
            recv_sem=sems.at[(1, *at)],
            device_id={"mesh": p},
            device_id_type=MESH,
        )

    q, r = me // QUAD, lax.rem(me, QUAD)
    high, low = r // 2, lax.rem(r, 2)
    near = [2 * high + 1 - low, 2 * (1 - high) + low, 2 * (1 - high) + 1 - low]

    def quad_at(t):
        return lax.rem(q + t, quads)

    def mid_copy(j, t, h):
        part = pl.ds(h * piece, piece)
        return to(
            far_send.at[j, t - 1, part],
            mid.at[j, t - 1, part],
            mid_sems,
            (j, t - 1, h),
            q * QUAD + near[j],
        )

    def near_copy(j):
        return to(near_send.at[j], near_recv.at[j], near_sems, (j,), q * QUAD + near[j])

    def far_copy(t, h):
        return to(
            summed.at[t - 1, h],
            far_recv.at[t - 1, pl.ds(h * piece, piece)],
            far_sems,
            (t - 1, h),
            quad_at(t) * QUAD + r,
        )

    def adm_copy(k):
        return to(adm_send, adm_recv.at[k - 1], adm_sems, (k - 1,), lax.rem(me + k, n))

    def grad_copy(k):
        return to(grad_send, grad_recv.at[k - 1], grad_sems, (k - 1,), lax.rem(me + k, n))

    def off_copy(side):
        return to(off_send, off_halo.at[side], off_sems, (side,), up if side == 0 else down)

    def halo_copy(solve, reach, side):
        mine = elems + (elems // 2 if (side == 0) == (reach == 0) else 0)
        there = mine - elems if side == 0 else mine + elems
        return to(
            ext.at[solve, pl.ds(mine, elems // 2)],
            ext.at[solve, pl.ds(there, elems // 2)],
            halo_sems,
            (solve, reach, side),
            up if side == 0 else down,
        )

    def each_side(copy, what, incoming):
        @pl.when(has_down if incoming else has_up)
        def _():
            getattr(copy(0), what)()

        @pl.when(has_up if incoming else has_down)
        def _():
            getattr(copy(1), what)()

    @pl.when(jnp.logical_not(has_down))
    def _():
        off_halo[0] = jnp.zeros((8, LANES), F32)
        for solve in range(2):
            ext[solve, 0:elems] = jnp.zeros((elems, width), BF16)

    @pl.when(jnp.logical_not(has_up))
    def _():
        off_halo[1] = jnp.zeros((8, LANES), F32)
        for solve in range(2):
            ext[solve, 2 * elems : 3 * elems] = jnp.zeros((elems, width), BF16)

    field_re[...] = jnp.zeros_like(field_re)
    field_im[...] = jnp.zeros_like(field_im)
    for load in loads[:3]:
        load.wait()
    target = owner_ref[...] * elems + slot_ref[...]

    def partial_sum(p):
        pick = (iota((elems, rows), 0) + p * elems) == target
        return dot(pick.astype(F32).astype(BF16), src_ref[...])

    for t in range(1, quads):
        for j in range(QUAD - 1):
            far_send[j, t - 1] = partial_sum(quad_at(t) * QUAD + near[j]).astype(BF16)

    depth = w_fwd.shape[0]
    over = depth - (FACES + 1) * nb

    def fold_forward():
        for load in loads[7:]:
            load.wait()
        inv_full[...] = full(inv_ref[...]).astype(BF16)

        @pl.loop(0, FACES)
        def _(f):
            at = pl.ds(pl.multiple_of(f * nb, nb), nb)
            w_fwd[at, :] = dot(coupling_ref[f], inv_full[...]).astype(BF16)

        w_fwd[FACES * nb : depth - over, :] = dot(liner_ref[...], inv_full[...]).astype(BF16)
        w_fwd[depth - over :, :] = jnp.zeros((over, width), BF16)
        w_adj[depth - over :, :] = jnp.zeros((over, width), BF16)

    sends_first = lax.rem(lax.axis_index("mode"), 2) == 0

    pl.semaphore_wait(barrier, n - 1)
    for h in range(pieces):
        for t in range(1, quads):
            for j in (2, 0, 1):
                mid_copy(j, t, h).start()
    for load in loads[3:7]:
        load.wait()
    off_send[...] = jnp.zeros_like(off_send)
    off_send[0:FACES, 0:elems] = off_ref[...].astype(F32)
    off_send[FACES : FACES + 1, 0:elems] = face_ref[...].astype(F32)
    off_send[FACES + 1 : FACES + 2, 0:elems] = weight_ref[...]
    adm_send[...] = jnp.zeros_like(adm_send)
    adm_send[0:2, 0:lin] = adm_ref[...]
    place = me * lin
    turned = pltpu.roll(adm_send[:, :LANES], lax.rem(place, LANES), 1)
    lane_f = iota((8, faces), 1)
    mine_f = jnp.logical_and(lane_f >= place, lane_f < place + lin)
    adm_send[...] = jnp.where(
        mine_f, jnp.concatenate([turned] * (faces // LANES), axis=1), 0.0
    )

    each_side(off_copy, "start", False)
    for k in range(1, n):
        adm_copy(k).start()
    for j in (2, 0, 1):
        near_send[j] = partial_sum(q * QUAD + near[j]).astype(BF16)
    near_copy(0).start()
    fold_forward()

    far_own = [partial_sum(quad_at(t) * QUAD + r) for t in range(1, quads)]
    for h in range(pieces):
        for t in range(1, quads):
            total = far_own[t - 1][h * piece : (h + 1) * piece]
            for j in (2, 0, 1):
                mid_copy(j, t, h).wait_recv()
                total = total + mid[j, t - 1, h * piece : (h + 1) * piece].astype(F32)
            summed[t - 1, h] = total.astype(BF16)
            far_copy(t, h).start()
    near_copy(2).start()
    near_copy(1).start()

    def fold_adjoint(f, matrix):
        turned = dot(inv_ref[...], full(matrix).astype(BF16))
        turned = jnp.concatenate([turned, jnp.zeros((wide - nb, width), F32)], axis=0).T
        rest = jnp.zeros((nb, width - wide), F32)
        re = jnp.concatenate([turned[:nb], rest], axis=1)
        im = jnp.concatenate([turned[nb:], rest], axis=1)
        at = pl.ds(f * nb if isinstance(f, int) else pl.multiple_of(f * nb, nb), nb)
        w_adj[at, :] = (re - swap(im)).astype(BF16)

    def fold_faces(begin, end):
        @pl.loop(begin, end)
        def _(f):
            fold_adjoint(f, coupling_ref[f])

    inv_herm[...] = full(inv_ref[...]).T.astype(BF16)
    liner_full[...] = full(liner_ref[...]).astype(BF16)
    fold_adjoint(FACES, liner_ref[...])
    fold_faces(0, FACES // 3)

    each_side(off_copy, "wait_recv", True)
    lane = iota((8, LANES), 1)
    offs = jnp.concatenate(
        [
            jnp.where(lane < elems, off_halo[0], pltpu.roll(off_send[...], elems, 1)),
            jnp.where(lane < elems, off_halo[1], 0.0),
        ],
        axis=1,
    )
    offs_col = jnp.concatenate([offs, jnp.zeros((LANES - 8, 2 * LANES), F32)], axis=0).T

    def picks(out_lo, count, in_lo):
        place = iota((count, LANES), 0) + (out_lo - in_lo) - iota((count, LANES), 1)
        place = place.astype(F32)
        cols = offs_col[out_lo : out_lo + count]
        here = offs if in_lo == 0 else pltpu.roll(offs, 2 * LANES - in_lo, 1)
        here = here[:, :LANES]

        def hot(x):
            return jnp.where(x, 1.0, 0.0).astype(BF16)

        fwd = [hot(place + cols[:, f : f + 1] == 0.0) for f in range(FACES)]
        adj = [hot(place == here[f : f + 1, :]) for f in range(FACES)]
        return fwd, adj

    half = (3 * elems - 2 * RIM) // 2
    for side in range(2):
        fwd, adj = picks(RIM + side * half, half, side * elems)
        for f in range(FACES):
            at = pl.ds((f % 2) * LANES, LANES)
            pick_fwd_ends[side, f // 2, :, at] = fwd[f]
            pick_adj_ends[side, f // 2, :, at] = adj[f]
    mid_rows = pick_fwd_mid.shape[1]
    mid_lo = elems - (mid_rows - elems) // 2
    fwd, adj = picks(mid_lo, mid_rows, elems // 2)
    for f in range(FACES):
        at = pl.ds((f % 2) * LANES, LANES)
        pick_fwd_mid[f // 2, :, at] = fwd[f]
        pick_adj_mid[f // 2, :, at] = adj[f]

    table = adm_send[...]
    for k in range(1, n):
        adm_copy(k).wait_recv()
        table = table + adm_recv[k - 1]
    face_all = offs_col[: 3 * elems, FACES : FACES + 1]
    weight = offs_col[elems : 2 * elems, FACES + 1 : FACES + 2]
    has_face = face_all == iota((3 * elems, faces), 1).astype(F32)
    y_re = jnp.sum(jnp.where(has_face, table[0:1], 0.0), axis=1, keepdims=True)
    y_im = jnp.sum(jnp.where(has_face, table[1:2], 0.0), axis=1, keepdims=True)
    own_face = offs_col[elems : 2 * elems, FACES : FACES + 1]
    own_face = own_face == iota((elems, faces), 1).astype(F32)

    admit_ref[0] = jnp.broadcast_to(y_re, (3 * elems, LANES))
    admit_ref[1] = jnp.broadcast_to(y_im, (3 * elems, LANES))
    admit_ref[2] = jnp.broadcast_to(-y_im, (3 * elems, LANES))
    split = nb // LANES * LANES

    def put(which, s, lo, value):
        count = value.shape[0]
        turned = swap(value)
        at, b = pl.ds(lo, count), s % 2
        is_re = iota((count, wide - split), 1) < nb - split

        def keep(ref, side, x):
            part = x[:, split:wide]
            if side == 0:
                ref[b, 0, at, 0:split] = x[:, :split].astype(BF16)
                ref[b, 0, at, split:wide] = jnp.where(is_re, part, 0.0).astype(BF16)
            else:
                ref[b, 1, at, split:wide] = jnp.where(is_re, 0.0, part).astype(BF16)
                ref[b, 1, at, wide:width] = x[:, wide:].astype(BF16)

        keep(field_re, 0, value)
        keep(field_re, 1, turned)
        keep(field_im, 0, turned)
        keep(field_im, 1, value)
        y_r = admit_ref[0, at]
        y_i = admit_ref[1 + which, at]
        for c in range(0, wide, LANES):
            re, im = value[:, c : c + LANES], turned[:, c : c + LANES]
            wall_re[b, at, c : c + LANES] = (y_r * re - y_i * im).astype(BF16)
            wall_im[b, at, c : c + LANES] = (y_r * im + y_i * re).astype(BF16)

    def rows_of(ref, spans):
        parts = [ref[lo:hi] for lo, hi in spans]
        return parts[0] if len(parts) == 1 else jnp.concatenate(parts, axis=0)

    def sweep(s, blocks, w_ref):
        b = (s - 1) % 2
        spans = [span for pieces, _ in blocks for _, _, span in pieces]

        parts = [[] for _ in range(FACES)]
        for pieces, taken in blocks:
            picked = [
                pick[i, lo - base : hi - base]
                for i in range(FACES // 2)
                for pick, base, (lo, hi) in pieces
            ]
            given = [
                jnp.concatenate([field[b, i, lo:hi] for i in range(2) for lo, hi in taken], axis=0)
                for field in (field_re, field_im)
            ]
            got = dot(jnp.concatenate(picked, axis=0), jnp.concatenate(given, axis=1)).astype(BF16)
            count = got.shape[0] // (FACES // 2)
            for i, part in enumerate(parts):
                row, lane = i % (FACES // 2) * count, i // (FACES // 2) * width
                part.append(got[row : row + count, lane : lane + width])
        met = [part[0] if len(part) == 1 else jnp.concatenate(part, axis=0) for part in parts]
        left = jnp.concatenate(
            [
                jnp.concatenate(met[: FACES // 2] + [rows_of(wall_re.at[b], spans)], axis=1),
                jnp.concatenate(met[FACES // 2 :] + [rows_of(wall_im.at[b], spans)], axis=1),
            ],
            axis=0,
        )
        prod = dot(left, w_ref[...])
        count = prod.shape[0] // 2
        rest = rows_of(start_ref, spans) - prod[:count]
        turned = swap(prod[count:])
        is_re = iota((count, wide - split), 1) < nb - split
        part = turned[:, split:wide]
        return jnp.concatenate(
            [
                rest[:, :split] + turned[:, :split],
                rest[:, split:wide] + jnp.where(is_re, part, -part),
                rest[:, wide:] - turned[:, wide:],
            ],
            axis=1,
        )

    def solve(which, start, ends, middle, w_ref, beside):
        ext[which, own] = start.astype(BF16)
        for reach in range(2):
            each_side(lambda side: halo_copy(which, reach, side), "start", False)
        start_ref[own] = start
        put(which, 0, elems, start)

        total = 3 * elems

        def lower(span):
            return (ends.at[0], RIM, span)

        def upper(span):
            return (ends.at[1], RIM + half, span)

        def centre(*spans):
            taken = (elems // 2, elems // 2 + LANES)
            return [(middle, mid_lo, span) for span in spans], [taken]

        def first_sweep(*blocks):
            now = sweep(1, blocks, w_ref)
            at = 0
            for lo, hi in [span for pieces, _ in blocks for _, _, span in pieces]:
                put(which, 1, lo, now[at : at + hi - lo])
                at += hi - lo

        def arrive(reach):
            each_side(lambda side: halo_copy(which, reach, side), "wait_recv", True)
            for lo in (elems // 2 * (1 - reach), 2 * elems + elems // 2 * reach):
                halo = ext[which, lo : lo + elems // 2].astype(F32)
                start_ref[lo : lo + elems // 2] = halo
                put(which, 0, lo, halo)

        inner, near_lo, far_lo = elems + RIM, elems // 2 + RIM, RIM
        beside()
        first_sweep(centre((inner, total - inner)))
        arrive(0)
        first_sweep(centre((near_lo, inner), (total - inner, total - near_lo)))
        arrive(1)
        outer = [lower((far_lo, near_lo)), upper((total - near_lo, total - far_lo))]
        first_sweep((outer, [(0, elems), (total - elems, total)]))
        for s in range(2, SWEEPS + 1):
            lo, hi = RIM * s, total - RIM * s
            if hi - lo > mid_rows:
                blocks = (
                    ([lower((lo, total // 2))], [(0, LANES)]),
                    ([upper((total // 2, hi))], [(total - LANES, total)]),
                )
            else:
                blocks = (centre((lo, hi)),)
            now = sweep(s, blocks, w_ref)
            if s < SWEEPS:
                put(which, s, lo, now)
        return now.astype(BF16)

    forcing = partial_sum(me)
    for j in (0, 1, 2):
        near_copy(j).wait_recv()
        forcing = forcing + near_recv[j].astype(F32)
    for t in range(1, quads):
        for h in range(pieces):
            far_copy(t, h).wait_recv()
        forcing = forcing + far_recv[t - 1].astype(F32)

    state = solve(
        0,
        dot(forcing.astype(BF16), inv_full[...]),
        pick_fwd_ends,
        pick_fwd_mid,
        w_fwd,
        lambda: fold_faces(FACES // 3, 2 * FACES // 3),
    )
    source = weight * state.astype(F32)

    def sent_halo(which):
        for reach in range(2):
            each_side(lambda side: halo_copy(which, reach, side), "wait_send", False)

    walls = []

    def beside():
        state_ref[...] = state
        walls.append(dot(state, liner_full[...]))
        fold_faces(2 * FACES // 3, FACES)
        for t in range(1, quads):
            for h in range(pieces):
                for j in range(QUAD - 1):
                    mid_copy(j, t, h).wait_send()
                far_copy(t, h).wait_send()
        for j in range(QUAD - 1):
            near_copy(j).wait_send()
        for k in range(1, n):
            adm_copy(k).wait_send()
        each_side(off_copy, "wait_send", False)
        sent_halo(0)

    adjoint = solve(
        1,
        dot(source.astype(BF16), inv_herm[...]),
        pick_adj_ends,
        pick_adj_mid,
        w_adj,
        beside,
    )
    adjoint_f = adjoint.astype(F32)
    wall = walls[0]
    term_re = jnp.sum(adjoint_f * wall, axis=1, keepdims=True) / -16.0
    term_im = jnp.sum(adjoint_f * times_i(wall), axis=1, keepdims=True) / -16.0
    grad_re = jnp.sum(jnp.where(own_face, term_re, 0.0), axis=0, keepdims=True)
    grad_im = jnp.sum(jnp.where(own_face, term_im, 0.0), axis=0, keepdims=True)
    total = jnp.concatenate([grad_re, grad_im, jnp.zeros((6, faces), F32)], axis=0)
    grad_send[...] = total
    for k in range(1, n):
        grad_copy(k).start()
    adjoint_ref[...] = adjoint
    for k in range(1, n):
        grad_copy(k).wait_recv()
        total = total + grad_recv[k - 1]
    total = jnp.where(mine_f, total, 0.0)
    parts = [total[:, i : i + LANES] for i in range(0, faces, LANES)]
    turned = pltpu.roll(sum(parts[1:], parts[0]), LANES - lax.rem(place, LANES), 1)
    grad_ref[...] = turned[0:2, 0:lin]

    for k in range(1, n):
        grad_copy(k).wait_send()
    sent_halo(1)


def finish(state_in, adjoint_in, grad_in, state_out, adjoint_out, grad_out, sems):
    pairs = ((state_in, state_out), (adjoint_in, adjoint_out), (grad_in, grad_out))
    moves = [pltpu.make_async_copy(a, b, sems.at[i]) for i, (a, b) in enumerate(pairs)]
    for move in moves:
        move.start()
    for move in moves:
        move.wait()


def solution(mesh):
    n = mesh.shape["mesh"]

    def local(
        src_rows,
        src_owner,
        src_slot,
        neighbour_offset,
        liner_face,
        admittance,
        observe_weight,
        coupling,
        block_inv,
        liner_op,
    ):
        rows, width = src_rows.shape
        nb = width // 2
        elems = liner_face.shape[0]
        lin = admittance.shape[1]
        faces = n * lin
        quads = n // QUAD
        pieces = 2
        wide = -(-nb // LANES) * LANES
        half = (3 * elems - 2 * RIM) // 2
        others = max(quads - 1, 1)
        vmem, dma = pltpu.VMEM, pltpu.SemaphoreType.DMA
        args = (
            src_owner.reshape(1, rows),
            src_slot.reshape(1, rows),
            neighbour_offset.T,
            liner_face.reshape(1, elems),
            admittance,
            observe_weight.reshape(1, elems),
            src_rows,
            coupling,
            block_inv,
            liner_op,
        )
        parts = pl.pallas_call(
            functools.partial(kernel, n),
            out_shape=(
                vmem((elems, width), BF16),
                vmem((elems, width), BF16),
                vmem((2, lin), F32),
            ),
            in_specs=[pl.BlockSpec(memory_space=pltpu.HBM)] * len(args),
            out_specs=(pl.BlockSpec(memory_space=pltpu.VMEM),) * 3,
            scratch_shapes=[vmem(x.shape, x.dtype) for x in args]
            + [
                dma((len(args),)),
                vmem((QUAD - 1, others, elems, width), BF16),
                vmem((QUAD - 1, elems, width), BF16),
                vmem((QUAD - 1, others, elems, width), BF16),
                vmem((others, pieces, elems // pieces, width), BF16),
                vmem((QUAD - 1, elems, width), BF16),
                vmem((others, elems, width), BF16),
                dma((2, QUAD - 1, others, pieces)),
                dma((2, QUAD - 1)),
                dma((2, others, pieces)),
                vmem((8, faces), F32),
                vmem((n - 1, 8, faces), F32),
                dma((2, n - 1)),
                vmem((8, LANES), F32),
                vmem((2, 8, LANES), F32),
                dma((2, 2)),
                vmem((8, faces), F32),
                vmem((n - 1, 8, faces), F32),
                dma((2, n - 1)),
                vmem((2, 3 * elems, width), BF16),
                dma((2, 2, 2, 2)),
                vmem((3 * elems, width), F32),
                vmem((2, 2, 3 * elems, width), BF16),
                vmem((2, 2, 3 * elems, width), BF16),
                vmem((2, 3 * elems, wide), BF16),
                vmem((2, 3 * elems, wide), BF16),
                vmem((width, width), BF16),
                vmem((width, width), BF16),
                vmem((width, width), BF16),
                vmem((FACES * nb + wide, width), BF16),
                vmem((FACES * nb + wide, width), BF16),
                vmem((2, FACES // 2, half, 2 * LANES), BF16),
                vmem((2, FACES // 2, half, 2 * LANES), BF16),
                vmem((FACES // 2, LANES - 2 * RIM, 2 * LANES), BF16),
                vmem((FACES // 2, LANES - 2 * RIM, 2 * LANES), BF16),
                vmem((3, 3 * elems, LANES), F32),
            ],
            compiler_params=pltpu.CompilerParams(
                collective_id=0, has_side_effects=True, vmem_limit_bytes=2**26 - 2**21
            ),
        )(*(pltpu.with_memory_space_constraint(x, pltpu.HBM) for x in args))
        anywhere = pl.BlockSpec(memory_space=pl.ANY)
        return tuple(
            pl.pallas_call(
                finish,
                out_shape=tuple(jax.ShapeDtypeStruct(x.shape, x.dtype) for x in parts),
                in_specs=[anywhere] * 3,
                out_specs=(anywhere,) * 3,
                scratch_shapes=[dma((3,))],
                compiler_params=pltpu.CompilerParams(vmem_limit_bytes=2**20),
            )(*parts)
        )

    placed = (
        P(("mode", "mesh"), None),
        P(("mode", "mesh"), None),
        P(("mode", "mesh")),
        P(("mode", "mesh"), None),
        P(("mode", "mesh")),
        P("mode", "mesh"),
        P(("mode", "mesh")),
        P("mode", None, None),
        P("mode", None),
        P("mode", None),
    )
    return jax.shard_map(
        local,
        mesh=mesh,
        in_specs=placed,
        out_specs=(P(("mode", "mesh"), None), P(("mode", "mesh"), None), P("mode", "mesh")),
        check_vma=False,
    )
```

```python
import functools

import jax
import jax.numpy as jnp
from jax import lax
from jax.experimental import pallas as pl
from jax.experimental.pallas import tpu as pltpu
from jax.sharding import PartitionSpec as P

SWEEPS = 4
RIM = 16
FACES = 6
QUAD = 4
LANES = 128
MESH = pl.DeviceIdType.MESH
F32 = jnp.float32
BF16 = jnp.bfloat16


def iota(shape, dim):
    return lax.broadcasted_iota(jnp.int32, shape, dim)


def dot(a, b):
    return jnp.dot(a, b, preferred_element_type=F32)


def swap(x):
    return pltpu.roll(x, x.shape[1] // 2, 1)


def first(x):
    return iota(x.shape, 1) < x.shape[1] // 2


def times_i(x):
    turned = swap(x)
    return jnp.where(first(x), -turned, turned)


def full(x):
    x = x.astype(F32)
    return jnp.concatenate([x, times_i(x)], axis=0)


def kernel(
    n,
    owner_hbm,
    slot_hbm,
    off_hbm,
    face_hbm,
    adm_hbm,
    weight_hbm,
    src_hbm,
    coupling_hbm,
    inv_hbm,
    liner_hbm,
    state_ref,
    adjoint_ref,
    grad_ref,
    owner_ref,
    slot_ref,
    off_ref,
    face_ref,
    adm_ref,
    weight_ref,
    src_ref,
    coupling_ref,
    inv_ref,
    liner_ref,
    load_sems,
    far_send,
    near_send,
    mid,
    summed,
    near_recv,
    far_recv,
    mid_sems,
    near_sems,
    far_sems,
    adm_send,
    adm_recv,
    adm_sems,
    off_send,
    off_halo,
    off_sems,
    grad_send,
    grad_recv,
    grad_sems,
    ext,
    halo_sems,
    start_ref,
    field_re,
    field_im,
    wall_re,
    wall_im,
    inv_full,
    inv_herm,
    liner_full,
    w_fwd,
    w_adj,
    pick_fwd_ends,
    pick_adj_ends,
    pick_fwd_mid,
    pick_adj_mid,
    admit_ref,
):
    me = lax.axis_index("mesh")
    elems = off_ref.shape[1]
    nb, width = inv_ref.shape
    lin = adm_ref.shape[1]
    rows = src_ref.shape[0]
    faces = adm_send.shape[1]
    wide = wall_re.shape[2]
    quads = n // QUAD
    pieces = summed.shape[1]
    piece = elems // pieces
    own = pl.ds(elems, elems)

    up, down = jnp.minimum(me + 1, n - 1), jnp.maximum(me - 1, 0)
    has_up, has_down = me < n - 1, me > 0

    barrier = pltpu.get_barrier_semaphore()
    for k in range(1, n):
        pl.semaphore_signal(
            barrier, inc=1, device_id={"mesh": lax.rem(me + k, n)}, device_id_type=MESH
        )

    loads = [
        pltpu.make_async_copy(hbm, here, load_sems.at[i])
        for i, (hbm, here) in enumerate(
            (
                (owner_hbm, owner_ref),
                (slot_hbm, slot_ref),
                (src_hbm, src_ref),
                (off_hbm, off_ref),
                (face_hbm, face_ref),
                (weight_hbm, weight_ref),
                (adm_hbm, adm_ref),
                (inv_hbm, inv_ref),
                (coupling_hbm, coupling_ref),
                (liner_hbm, liner_ref),
            )
        )
    ]
    for load in loads:
        load.start()

    def to(src, dst, sems, at, p):
        return pltpu.make_async_remote_copy(
            src_ref=src,
            dst_ref=dst,
            send_sem=sems.at[(0, *at)],
            recv_sem=sems.at[(1, *at)],
            device_id={"mesh": p},
            device_id_type=MESH,
        )

    q, r = me // QUAD, lax.rem(me, QUAD)
    high, low = r // 2, lax.rem(r, 2)
    near = [2 * high + 1 - low, 2 * (1 - high) + low, 2 * (1 - high) + 1 - low]

    def quad_at(t):
        return lax.rem(q + t, quads)

    def mid_copy(j, t, h):
        part = pl.ds(h * piece, piece)
        return to(
            far_send.at[j, t - 1, part],
            mid.at[j, t - 1, part],
            mid_sems,
            (j, t - 1, h),
            q * QUAD + near[j],
        )

    def near_copy(j):
        return to(near_send.at[j], near_recv.at[j], near_sems, (j,), q * QUAD + near[j])

    def far_copy(t, h):
        return to(
            summed.at[t - 1, h],
            far_recv.at[t - 1, pl.ds(h * piece, piece)],
            far_sems,
            (t - 1, h),
            quad_at(t) * QUAD + r,
        )

    def adm_copy(k):
        return to(adm_send, adm_recv.at[k - 1], adm_sems, (k - 1,), lax.rem(me + k, n))

    def grad_copy(k):
        return to(grad_send, grad_recv.at[k - 1], grad_sems, (k - 1,), lax.rem(me + k, n))

    def off_copy(side):
        return to(off_send, off_halo.at[side], off_sems, (side,), up if side == 0 else down)

    def halo_copy(solve, reach, side):
        mine = elems + (elems // 2 if (side == 0) == (reach == 0) else 0)
        there = mine - elems if side == 0 else mine + elems
        return to(
            ext.at[solve, pl.ds(mine, elems // 2)],
            ext.at[solve, pl.ds(there, elems // 2)],
            halo_sems,
            (solve, reach, side),
            up if side == 0 else down,
        )

    def each_side(copy, what, incoming):
        @pl.when(has_down if incoming else has_up)
        def _():
            getattr(copy(0), what)()

        @pl.when(has_up if incoming else has_down)
        def _():
            getattr(copy(1), what)()

    @pl.when(jnp.logical_not(has_down))
    def _():
        off_halo[0] = jnp.zeros((8, LANES), F32)
        for solve in range(2):
            ext[solve, 0:elems] = jnp.zeros((elems, width), BF16)

    @pl.when(jnp.logical_not(has_up))
    def _():
        off_halo[1] = jnp.zeros((8, LANES), F32)
        for solve in range(2):
            ext[solve, 2 * elems : 3 * elems] = jnp.zeros((elems, width), BF16)

    field_re[...] = jnp.zeros_like(field_re)
    field_im[...] = jnp.zeros_like(field_im)
    for load in loads[:3]:
        load.wait()
    target = owner_ref[...] * elems + slot_ref[...]

    def partial_sums(owners):
        picks = [(iota((elems, rows), 0) + p * elems) == target for p in owners]
        picks = [pick.astype(F32).astype(BF16) for pick in picks]
        got = dot(jnp.concatenate(picks, axis=0), src_ref[...])
        return [got[i * elems : (i + 1) * elems] for i in range(len(owners))]

    for t in range(1, quads):
        got = partial_sums([quad_at(t) * QUAD + near[j] for j in range(QUAD - 1)])
        for j in range(QUAD - 1):
            far_send[j, t - 1] = got[j].astype(BF16)

    depth = w_fwd.shape[0]
    over = depth - (FACES + 1) * nb

    def fold_forward():
        for load in loads[7:]:
            load.wait()
        inv_full[...] = full(inv_ref[...]).astype(BF16)

        @pl.loop(0, FACES)
        def _(f):
            at = pl.ds(pl.multiple_of(f * nb, nb), nb)
            w_fwd[at, :] = dot(coupling_ref[f], inv_full[...]).astype(BF16)

        w_fwd[FACES * nb : depth - over, :] = dot(liner_ref[...], inv_full[...]).astype(BF16)
        w_fwd[depth - over :, :] = jnp.zeros((over, width), BF16)
        w_adj[depth - over :, :] = jnp.zeros((over, width), BF16)

    sends_first = lax.rem(lax.axis_index("mode"), 2) == 0

    pl.semaphore_wait(barrier, n - 1)
    for h in range(pieces):
        for t in range(1, quads):
            for j in (2, 0, 1):
                mid_copy(j, t, h).start()
    for load in loads[3:7]:
        load.wait()
    off_send[...] = jnp.zeros_like(off_send)
    off_send[0:FACES, 0:elems] = off_ref[...].astype(F32)
    off_send[FACES : FACES + 1, 0:elems] = face_ref[...].astype(F32)
    off_send[FACES + 1 : FACES + 2, 0:elems] = weight_ref[...]
    adm_send[...] = jnp.zeros_like(adm_send)
    adm_send[0:2, 0:lin] = adm_ref[...]
    place = me * lin
    turned = pltpu.roll(adm_send[:, :LANES], lax.rem(place, LANES), 1)
    lane_f = iota((8, faces), 1)
    mine_f = jnp.logical_and(lane_f >= place, lane_f < place + lin)
    adm_send[...] = jnp.where(
        mine_f, jnp.concatenate([turned] * (faces // LANES), axis=1), 0.0
    )

    each_side(off_copy, "start", False)
    for k in range(1, n):
        adm_copy(k).start()
    got = partial_sums([q * QUAD + near[j] for j in range(QUAD - 1)])
    for j in range(QUAD - 1):
        near_send[j] = got[j].astype(BF16)
    near_copy(2).start()
    near_copy(0).start()
    fold_forward()

    forcing, *far_own = partial_sums([me] + [quad_at(t) * QUAD + r for t in range(1, quads)])
    for h in range(pieces):
        for t in range(1, quads):
            total = far_own[t - 1][h * piece : (h + 1) * piece]
            for j in (2, 0, 1):
                mid_copy(j, t, h).wait_recv()
                total = total + mid[j, t - 1, h * piece : (h + 1) * piece].astype(F32)
            summed[t - 1, h] = total.astype(BF16)
            far_copy(t, h).start()
    near_copy(1).start()

    def fold_adjoint(f, matrix):
        turned = dot(inv_ref[...], full(matrix).astype(BF16))
        turned = jnp.concatenate([turned, jnp.zeros((wide - nb, width), F32)], axis=0).T
        rest = jnp.zeros((nb, width - wide), F32)
        re = jnp.concatenate([turned[:nb], rest], axis=1)
        im = jnp.concatenate([turned[nb:], rest], axis=1)
        at = pl.ds(f * nb if isinstance(f, int) else pl.multiple_of(f * nb, nb), nb)
        w_adj[at, :] = (re - swap(im)).astype(BF16)

    def fold_faces(begin, end):
        @pl.loop(begin, end)
        def _(f):
            fold_adjoint(f, coupling_ref[f])

    inv_herm[...] = full(inv_ref[...]).T.astype(BF16)
    liner_full[...] = full(liner_ref[...]).astype(BF16)
    fold_adjoint(FACES, liner_ref[...])
    fold_faces(0, FACES // 3)

    each_side(off_copy, "wait_recv", True)
    lane = iota((8, LANES), 1)
    offs = jnp.concatenate(
        [
            jnp.where(lane < elems, off_halo[0], pltpu.roll(off_send[...], elems, 1)),
            jnp.where(lane < elems, off_halo[1], 0.0),
        ],
        axis=1,
    )
    offs_col = jnp.concatenate([offs, jnp.zeros((LANES - 8, 2 * LANES), F32)], axis=0).T

    def picks(out_lo, count, in_lo):
        place = iota((count, LANES), 0) + (out_lo - in_lo) - iota((count, LANES), 1)
        place = place.astype(F32)
        cols = offs_col[out_lo : out_lo + count]
        here = offs if in_lo == 0 else pltpu.roll(offs, 2 * LANES - in_lo, 1)
        here = here[:, :LANES]

        def hot(x):
            return jnp.where(x, 1.0, 0.0).astype(BF16)

        fwd = [hot(place + cols[:, f : f + 1] == 0.0) for f in range(FACES)]
        adj = [hot(place == here[f : f + 1, :]) for f in range(FACES)]
        return fwd, adj

    half = (3 * elems - 2 * RIM) // 2
    for side in range(2):
        fwd, adj = picks(RIM + side * half, half, side * elems)
        for f in range(FACES):
            at = pl.ds((f % 2) * LANES, LANES)
            pick_fwd_ends[side, f // 2, :, at] = fwd[f]
            pick_adj_ends[side, f // 2, :, at] = adj[f]
    mid_rows = pick_fwd_mid.shape[1]
    mid_lo = elems - (mid_rows - elems) // 2
    fwd, adj = picks(mid_lo, mid_rows, elems // 2)
    for f in range(FACES):
        at = pl.ds((f % 2) * LANES, LANES)
        pick_fwd_mid[f // 2, :, at] = fwd[f]
        pick_adj_mid[f // 2, :, at] = adj[f]

    table = adm_send[...]
    for k in range(1, n):
        adm_copy(k).wait_recv()
        table = table + adm_recv[k - 1]
    face_all = offs_col[: 3 * elems, FACES : FACES + 1]
    weight = offs_col[elems : 2 * elems, FACES + 1 : FACES + 2]
    has_face = face_all == iota((3 * elems, faces), 1).astype(F32)
    y_re = jnp.sum(jnp.where(has_face, table[0:1], 0.0), axis=1, keepdims=True)
    y_im = jnp.sum(jnp.where(has_face, table[1:2], 0.0), axis=1, keepdims=True)
    own_face = offs_col[elems : 2 * elems, FACES : FACES + 1]
    own_face = own_face == iota((elems, faces), 1).astype(F32)

    admit_ref[0] = jnp.broadcast_to(y_re, (3 * elems, LANES))
    admit_ref[1] = jnp.broadcast_to(y_im, (3 * elems, LANES))
    admit_ref[2] = jnp.broadcast_to(-y_im, (3 * elems, LANES))
    split = nb // LANES * LANES

    def put(which, s, lo, value):
        count = value.shape[0]
        turned = swap(value)
        at, b = pl.ds(lo, count), s % 2
        is_re = iota((count, wide - split), 1) < nb - split

        def keep(ref, side, x):
            part = x[:, split:wide]
            if side == 0:
                ref[b, 0, at, 0:split] = x[:, :split].astype(BF16)
                ref[b, 0, at, split:wide] = jnp.where(is_re, part, 0.0).astype(BF16)
            else:
                ref[b, 1, at, split:wide] = jnp.where(is_re, 0.0, part).astype(BF16)
                ref[b, 1, at, wide:width] = x[:, wide:].astype(BF16)

        keep(field_re, 0, value)
        keep(field_re, 1, turned)
        keep(field_im, 0, turned)
        keep(field_im, 1, value)
        y_r = admit_ref[0, at]
        y_i = admit_ref[1 + which, at]
        for c in range(0, wide, LANES):
            re, im = value[:, c : c + LANES], turned[:, c : c + LANES]
            wall_re[b, at, c : c + LANES] = (y_r * re - y_i * im).astype(BF16)
            wall_im[b, at, c : c + LANES] = (y_r * im + y_i * re).astype(BF16)

    def rows_of(ref, spans):
        parts = [ref[lo:hi] for lo, hi in spans]
        return parts[0] if len(parts) == 1 else jnp.concatenate(parts, axis=0)

    def sweep(s, blocks, w_ref):
        b = (s - 1) % 2
        spans = [span for pieces, _ in blocks for _, _, span in pieces]

        parts = [[] for _ in range(FACES)]
        for pieces, taken in blocks:
            picked = [
                pick[i, lo - base : hi - base]
                for i in range(FACES // 2)
                for pick, base, (lo, hi) in pieces
            ]
            given = [
                jnp.concatenate([field[b, i, lo:hi] for i in range(2) for lo, hi in taken], axis=0)
                for field in (field_re, field_im)
            ]
            got = dot(jnp.concatenate(picked, axis=0), jnp.concatenate(given, axis=1)).astype(BF16)
            count = got.shape[0] // (FACES // 2)
            for i, part in enumerate(parts):
                row, lane = i % (FACES // 2) * count, i // (FACES // 2) * width
                part.append(got[row : row + count, lane : lane + width])
        met = [part[0] if len(part) == 1 else jnp.concatenate(part, axis=0) for part in parts]
        left = jnp.concatenate(
            [
                jnp.concatenate(met[: FACES // 2] + [rows_of(wall_re.at[b], spans)], axis=1),
                jnp.concatenate(met[FACES // 2 :] + [rows_of(wall_im.at[b], spans)], axis=1),
            ],
            axis=0,
        )
        prod = dot(left, w_ref[...])
        count = prod.shape[0] // 2
        rest = rows_of(start_ref, spans) - prod[:count]
        turned = swap(prod[count:])
        is_re = iota((count, wide - split), 1) < nb - split
        part = turned[:, split:wide]
        return jnp.concatenate(
            [
                rest[:, :split] + turned[:, :split],
                rest[:, split:wide] + jnp.where(is_re, part, -part),
                rest[:, wide:] - turned[:, wide:],
            ],
            axis=1,
        )

    def solve(which, start, ends, middle, w_ref, beside):
        ext[which, own] = start.astype(BF16)
        for reach in range(2):
            each_side(lambda side: halo_copy(which, reach, side), "start", False)
        start_ref[own] = start
        put(which, 0, elems, start)

        total = 3 * elems

        def lower(span):
            return (ends.at[0], RIM, span)

        def upper(span):
            return (ends.at[1], RIM + half, span)

        def centre(*spans):
            taken = (elems // 2, elems // 2 + LANES)
            return [(middle, mid_lo, span) for span in spans], [taken]

        def first_sweep(*blocks):
            now = sweep(1, blocks, w_ref)
            at = 0
            for lo, hi in [span for pieces, _ in blocks for _, _, span in pieces]:
                put(which, 1, lo, now[at : at + hi - lo])
                at += hi - lo

        def arrive(reach):
            each_side(lambda side: halo_copy(which, reach, side), "wait_recv", True)
            for lo in (elems // 2 * (1 - reach), 2 * elems + elems // 2 * reach):
                halo = ext[which, lo : lo + elems // 2].astype(F32)
                start_ref[lo : lo + elems // 2] = halo
                put(which, 0, lo, halo)

        inner, near_lo, far_lo = elems + RIM, elems // 2 + RIM, RIM
        beside()
        first_sweep(centre((inner, total - inner)))
        arrive(0)
        first_sweep(centre((near_lo, inner), (total - inner, total - near_lo)))
        arrive(1)
        outer = [lower((far_lo, near_lo)), upper((total - near_lo, total - far_lo))]
        first_sweep((outer, [(0, elems), (total - elems, total)]))
        for s in range(2, SWEEPS + 1):
            lo, hi = RIM * s, total - RIM * s
            if hi - lo > mid_rows:
                blocks = (
                    ([lower((lo, total // 2))], [(0, LANES)]),
                    ([upper((total // 2, hi))], [(total - LANES, total)]),
                )
            else:
                blocks = (centre((lo, hi)),)
            now = sweep(s, blocks, w_ref)
            if s < SWEEPS:
                put(which, s, lo, now)
        return now.astype(BF16)

    for j in (0, 1, 2):
        near_copy(j).wait_recv()
        forcing = forcing + near_recv[j].astype(F32)
    for t in range(1, quads):
        for h in range(pieces):
            far_copy(t, h).wait_recv()
        forcing = forcing + far_recv[t - 1].astype(F32)

    state = solve(
        0,
        dot(forcing.astype(BF16), inv_full[...]),
        pick_fwd_ends,
        pick_fwd_mid,
        w_fwd,
        lambda: fold_faces(FACES // 3, 2 * FACES // 3),
    )
    source = weight * state.astype(F32)

    def sent_halo(which):
        for reach in range(2):
            each_side(lambda side: halo_copy(which, reach, side), "wait_send", False)

    walls = []

    def beside():
        state_ref[...] = state
        walls.append(dot(state, liner_full[...]))
        fold_faces(2 * FACES // 3, FACES)
        for t in range(1, quads):
            for h in range(pieces):
                for j in range(QUAD - 1):
                    mid_copy(j, t, h).wait_send()
                far_copy(t, h).wait_send()
        for j in range(QUAD - 1):
            near_copy(j).wait_send()
        for k in range(1, n):
            adm_copy(k).wait_send()
        each_side(off_copy, "wait_send", False)
        sent_halo(0)

    adjoint = solve(
        1,
        dot(source.astype(BF16), inv_herm[...]),
        pick_adj_ends,
        pick_adj_mid,
        w_adj,
        beside,
    )
    adjoint_f = adjoint.astype(F32)
    wall = walls[0]
    term_re = jnp.sum(adjoint_f * wall, axis=1, keepdims=True) / -16.0
    term_im = jnp.sum(adjoint_f * times_i(wall), axis=1, keepdims=True) / -16.0
    grad_re = jnp.sum(jnp.where(own_face, term_re, 0.0), axis=0, keepdims=True)
    grad_im = jnp.sum(jnp.where(own_face, term_im, 0.0), axis=0, keepdims=True)
    total = jnp.concatenate([grad_re, grad_im, jnp.zeros((6, faces), F32)], axis=0)
    grad_send[...] = total
    for k in range(1, n):
        grad_copy(k).start()
    adjoint_ref[...] = adjoint
    for k in range(1, n):
        grad_copy(k).wait_recv()
        total = total + grad_recv[k - 1]
    total = jnp.where(mine_f, total, 0.0)
    parts = [total[:, i : i + LANES] for i in range(0, faces, LANES)]
    turned = pltpu.roll(sum(parts[1:], parts[0]), LANES - lax.rem(place, LANES), 1)
    grad_ref[...] = turned[0:2, 0:lin]

    for k in range(1, n):
        grad_copy(k).wait_send()
    sent_halo(1)


def finish(state_in, adjoint_in, grad_in, state_out, adjoint_out, grad_out, sems):
    pairs = ((state_in, state_out), (adjoint_in, adjoint_out), (grad_in, grad_out))
    moves = [pltpu.make_async_copy(a, b, sems.at[i]) for i, (a, b) in enumerate(pairs)]
    for move in moves:
        move.start()
    for move in moves:
        move.wait()


def solution(mesh):
    n = mesh.shape["mesh"]

    def local(
        src_rows,
        src_owner,
        src_slot,
        neighbour_offset,
        liner_face,
        admittance,
        observe_weight,
        coupling,
        block_inv,
        liner_op,
    ):
        rows, width = src_rows.shape
        nb = width // 2
        elems = liner_face.shape[0]
        lin = admittance.shape[1]
        faces = n * lin
        quads = n // QUAD
        pieces = 2
        wide = -(-nb // LANES) * LANES
        half = (3 * elems - 2 * RIM) // 2
        others = max(quads - 1, 1)
        vmem, dma = pltpu.VMEM, pltpu.SemaphoreType.DMA
        args = (
            src_owner.reshape(1, rows),
            src_slot.reshape(1, rows),
            neighbour_offset.T,
            liner_face.reshape(1, elems),
            admittance,
            observe_weight.reshape(1, elems),
            src_rows,
            coupling,
            block_inv,
            liner_op,
        )
        parts = pl.pallas_call(
            functools.partial(kernel, n),
            out_shape=(
                vmem((elems, width), BF16),
                vmem((elems, width), BF16),
                vmem((2, lin), F32),
            ),
            in_specs=[pl.BlockSpec(memory_space=pltpu.HBM)] * len(args),
            out_specs=(pl.BlockSpec(memory_space=pltpu.VMEM),) * 3,
            scratch_shapes=[vmem(x.shape, x.dtype) for x in args]
            + [
                dma((len(args),)),
                vmem((QUAD - 1, others, elems, width), BF16),
                vmem((QUAD - 1, elems, width), BF16),
                vmem((QUAD - 1, others, elems, width), BF16),
                vmem((others, pieces, elems // pieces, width), BF16),
                vmem((QUAD - 1, elems, width), BF16),
                vmem((others, elems, width), BF16),
                dma((2, QUAD - 1, others, pieces)),
                dma((2, QUAD - 1)),
                dma((2, others, pieces)),
                vmem((8, faces), F32),
                vmem((n - 1, 8, faces), F32),
                dma((2, n - 1)),
                vmem((8, LANES), F32),
                vmem((2, 8, LANES), F32),
                dma((2, 2)),
                vmem((8, faces), F32),
                vmem((n - 1, 8, faces), F32),
                dma((2, n - 1)),
                vmem((2, 3 * elems, width), BF16),
                dma((2, 2, 2, 2)),
                vmem((3 * elems, width), F32),
                vmem((2, 2, 3 * elems, width), BF16),
                vmem((2, 2, 3 * elems, width), BF16),
                vmem((2, 3 * elems, wide), BF16),
                vmem((2, 3 * elems, wide), BF16),
                vmem((width, width), BF16),
                vmem((width, width), BF16),
                vmem((width, width), BF16),
                vmem((FACES * nb + wide, width), BF16),
                vmem((FACES * nb + wide, width), BF16),
                vmem((2, FACES // 2, half, 2 * LANES), BF16),
                vmem((2, FACES // 2, half, 2 * LANES), BF16),
                vmem((FACES // 2, LANES - 2 * RIM, 2 * LANES), BF16),
                vmem((FACES // 2, LANES - 2 * RIM, 2 * LANES), BF16),
                vmem((3, 3 * elems, LANES), F32),
            ],
            compiler_params=pltpu.CompilerParams(
                collective_id=0, has_side_effects=True, vmem_limit_bytes=2**26 - 2**21
            ),
        )(*(pltpu.with_memory_space_constraint(x, pltpu.HBM) for x in args))
        anywhere = pl.BlockSpec(memory_space=pl.ANY)
        return tuple(
            pl.pallas_call(
                finish,
                out_shape=tuple(jax.ShapeDtypeStruct(x.shape, x.dtype) for x in parts),
                in_specs=[anywhere] * 3,
                out_specs=(anywhere,) * 3,
                scratch_shapes=[dma((3,))],
                compiler_params=pltpu.CompilerParams(vmem_limit_bytes=2**20),
            )(*parts)
        )

    placed = (
        P(("mode", "mesh"), None),
        P(("mode", "mesh"), None),
        P(("mode", "mesh")),
        P(("mode", "mesh"), None),
        P(("mode", "mesh")),
        P("mode", "mesh"),
        P(("mode", "mesh")),
        P("mode", None, None),
        P("mode", None),
        P("mode", None),
    )
    return jax.shard_map(
        local,
        mesh=mesh,
        in_specs=placed,
        out_specs=(P(("mode", "mesh"), None), P(("mode", "mesh"), None), P("mode", "mesh")),
        check_vma=False,
    )
```

```python
import functools

import jax
import jax.numpy as jnp
from jax import lax
from jax.experimental import pallas as pl
from jax.experimental.pallas import tpu as pltpu
from jax.sharding import PartitionSpec as P

SWEEPS = 4
RIM = 16
FACES = 6
QUAD = 4
LANES = 128
MESH = pl.DeviceIdType.MESH
F32 = jnp.float32
BF16 = jnp.bfloat16


def iota(shape, dim):
    return lax.broadcasted_iota(jnp.int32, shape, dim)


def dot(a, b):
    return jnp.dot(a, b, preferred_element_type=F32)


def swap(x):
    return pltpu.roll(x, x.shape[1] // 2, 1)


def first(x):
    return iota(x.shape, 1) < x.shape[1] // 2


def times_i(x):
    turned = swap(x)
    return jnp.where(first(x), -turned, turned)


def full(x):
    x = x.astype(F32)
    return jnp.concatenate([x, times_i(x)], axis=0)


def kernel(
    n,
    owner_hbm,
    slot_hbm,
    off_hbm,
    face_hbm,
    adm_hbm,
    weight_hbm,
    src_hbm,
    coupling_hbm,
    inv_hbm,
    liner_hbm,
    state_ref,
    adjoint_ref,
    grad_ref,
    owner_ref,
    slot_ref,
    off_ref,
    face_ref,
    adm_ref,
    weight_ref,
    src_ref,
    coupling_ref,
    inv_ref,
    liner_ref,
    load_sems,
    far_send,
    near_send,
    mid,
    summed,
    near_recv,
    far_recv,
    mid_sems,
    near_sems,
    far_sems,
    adm_send,
    adm_recv,
    adm_sems,
    off_send,
    off_halo,
    off_sems,
    grad_send,
    grad_recv,
    grad_sems,
    ext,
    halo_sems,
    start_ref,
    field_re,
    field_im,
    wall_re,
    wall_im,
    inv_full,
    inv_herm,
    liner_full,
    w_fwd,
    w_adj,
    pick_fwd_ends,
    pick_adj_ends,
    pick_fwd_mid,
    pick_adj_mid,
    admit_ref,
):
    me = lax.axis_index("mesh")
    elems = off_ref.shape[1]
    nb, width = inv_ref.shape
    lin = adm_ref.shape[1]
    rows = src_ref.shape[0]
    faces = adm_send.shape[1]
    wide = wall_re.shape[2]
    quads = n // QUAD
    pieces = summed.shape[1]
    piece = elems // pieces
    own = pl.ds(elems, elems)

    up, down = jnp.minimum(me + 1, n - 1), jnp.maximum(me - 1, 0)
    has_up, has_down = me < n - 1, me > 0

    barrier = pltpu.get_barrier_semaphore()
    for k in range(1, n):
        pl.semaphore_signal(
            barrier, inc=1, device_id={"mesh": lax.rem(me + k, n)}, device_id_type=MESH
        )

    loads = [
        pltpu.make_async_copy(hbm, here, load_sems.at[i])
        for i, (hbm, here) in enumerate(
            (
                (owner_hbm, owner_ref),
                (slot_hbm, slot_ref),
                (src_hbm, src_ref),
                (off_hbm, off_ref),
                (face_hbm, face_ref),
                (weight_hbm, weight_ref),
                (adm_hbm, adm_ref),
                (inv_hbm, inv_ref),
                (coupling_hbm, coupling_ref),
                (liner_hbm, liner_ref),
            )
        )
    ]
    for load in loads:
        load.start()

    def to(src, dst, sems, at, p):
        return pltpu.make_async_remote_copy(
            src_ref=src,
            dst_ref=dst,
            send_sem=sems.at[(0, *at)],
            recv_sem=sems.at[(1, *at)],
            device_id={"mesh": p},
            device_id_type=MESH,
        )

    q, r = me // QUAD, lax.rem(me, QUAD)
    high, low = r // 2, lax.rem(r, 2)
    near = [2 * high + 1 - low, 2 * (1 - high) + low, 2 * (1 - high) + 1 - low]

    def quad_at(t):
        return lax.rem(q + t, quads)

    def mid_copy(j, t, h):
        part = pl.ds(h * piece, piece)
        return to(
            far_send.at[j, t - 1, part],
            mid.at[j, t - 1, part],
            mid_sems,
            (j, t - 1, h),
            q * QUAD + near[j],
        )

    def near_copy(j):
        return to(near_send.at[j], near_recv.at[j], near_sems, (j,), q * QUAD + near[j])

    def far_copy(t, h):
        return to(
            summed.at[t - 1, h],
            far_recv.at[t - 1, pl.ds(h * piece, piece)],
            far_sems,
            (t - 1, h),
            quad_at(t) * QUAD + r,
        )

    def adm_copy(k):
        return to(adm_send, adm_recv.at[k - 1], adm_sems, (k - 1,), lax.rem(me + k, n))

    def grad_copy(k):
        return to(grad_send, grad_recv.at[k - 1], grad_sems, (k - 1,), lax.rem(me + k, n))

    def off_copy(side):
        return to(off_send, off_halo.at[side], off_sems, (side,), up if side == 0 else down)

    def halo_copy(solve, reach, side):
        mine = elems + (elems // 2 if (side == 0) == (reach == 0) else 0)
        there = mine - elems if side == 0 else mine + elems
        return to(
            ext.at[solve, pl.ds(mine, elems // 2)],
            ext.at[solve, pl.ds(there, elems // 2)],
            halo_sems,
            (solve, reach, side),
            up if side == 0 else down,
        )

    def each_side(copy, what, incoming):
        @pl.when(has_down if incoming else has_up)
        def _():
            getattr(copy(0), what)()

        @pl.when(has_up if incoming else has_down)
        def _():
            getattr(copy(1), what)()

    @pl.when(jnp.logical_not(has_down))
    def _():
        off_halo[0] = jnp.zeros((8, LANES), F32)
        for solve in range(2):
            ext[solve, 0:elems] = jnp.zeros((elems, width), BF16)

    @pl.when(jnp.logical_not(has_up))
    def _():
        off_halo[1] = jnp.zeros((8, LANES), F32)
        for solve in range(2):
            ext[solve, 2 * elems : 3 * elems] = jnp.zeros((elems, width), BF16)

    field_re[...] = jnp.zeros_like(field_re)
    field_im[...] = jnp.zeros_like(field_im)
    for load in loads[:3]:
        load.wait()
    target = owner_ref[...] * elems + slot_ref[...]

    def partial_sums(owners):
        picks = [(iota((elems, rows), 0) + p * elems) == target for p in owners]
        picks = [pick.astype(F32).astype(BF16) for pick in picks]
        got = dot(jnp.concatenate(picks, axis=0), src_ref[...])
        return [got[i * elems : (i + 1) * elems] for i in range(len(owners))]

    for t in range(1, quads):
        got = partial_sums([quad_at(t) * QUAD + near[j] for j in range(QUAD - 1)])
        for j in range(QUAD - 1):
            far_send[j, t - 1] = got[j].astype(BF16)

    depth = w_fwd.shape[0]
    over = depth - (FACES + 1) * nb

    def fold_forward():
        for load in loads[7:]:
            load.wait()
        inv_full[...] = full(inv_ref[...]).astype(BF16)

        @pl.loop(0, FACES)
        def _(f):
            at = pl.ds(pl.multiple_of(f * nb, nb), nb)
            w_fwd[at, :] = dot(coupling_ref[f], inv_full[...]).astype(BF16)

        w_fwd[FACES * nb : depth - over, :] = dot(liner_ref[...], inv_full[...]).astype(BF16)
        w_fwd[depth - over :, :] = jnp.zeros((over, width), BF16)
        w_adj[depth - over :, :] = jnp.zeros((over, width), BF16)

    sends_first = lax.rem(lax.axis_index("mode"), 2) == 0

    pl.semaphore_wait(barrier, n - 1)
    for h in range(pieces):
        for t in range(1, quads):
            for j in (2, 0, 1):
                mid_copy(j, t, h).start()
    for load in loads[3:7]:
        load.wait()
    off_send[...] = jnp.zeros_like(off_send)
    off_send[0:FACES, 0:elems] = off_ref[...].astype(F32)
    off_send[FACES : FACES + 1, 0:elems] = face_ref[...].astype(F32)
    off_send[FACES + 1 : FACES + 2, 0:elems] = weight_ref[...]
    adm_send[...] = jnp.zeros_like(adm_send)
    adm_send[0:2, 0:lin] = adm_ref[...]
    place = me * lin
    turned = pltpu.roll(adm_send[:, :LANES], lax.rem(place, LANES), 1)
    lane_f = iota((8, faces), 1)
    mine_f = jnp.logical_and(lane_f >= place, lane_f < place + lin)
    adm_send[...] = jnp.where(
        mine_f, jnp.concatenate([turned] * (faces // LANES), axis=1), 0.0
    )

    got = partial_sums([q * QUAD + near[j] for j in range(QUAD - 1)])
    for j in range(QUAD - 1):
        near_send[j] = got[j].astype(BF16)
    near_copy(2).start()
    near_copy(0).start()
    each_side(off_copy, "start", False)
    for k in range(1, n):
        adm_copy(k).start()
    fold_forward()

    forcing, *far_own = partial_sums([me] + [quad_at(t) * QUAD + r for t in range(1, quads)])
    for h in range(pieces):
        for t in range(1, quads):
            total = far_own[t - 1][h * piece : (h + 1) * piece]
            for j in (2, 0, 1):
                mid_copy(j, t, h).wait_recv()
                total = total + mid[j, t - 1, h * piece : (h + 1) * piece].astype(F32)
            summed[t - 1, h] = total.astype(BF16)
            far_copy(t, h).start()
    near_copy(1).start()

    def fold_adjoint(f, matrix):
        turned = dot(inv_ref[...], full(matrix).astype(BF16))
        turned = jnp.concatenate([turned, jnp.zeros((wide - nb, width), F32)], axis=0).T
        rest = jnp.zeros((nb, width - wide), F32)
        re = jnp.concatenate([turned[:nb], rest], axis=1)
        im = jnp.concatenate([turned[nb:], rest], axis=1)
        at = pl.ds(f * nb if isinstance(f, int) else pl.multiple_of(f * nb, nb), nb)
        w_adj[at, :] = (re - swap(im)).astype(BF16)

    def fold_faces(begin, end):
        @pl.loop(begin, end)
        def _(f):
            fold_adjoint(f, coupling_ref[f])

    inv_herm[...] = full(inv_ref[...]).T.astype(BF16)
    liner_full[...] = full(liner_ref[...]).astype(BF16)
    fold_adjoint(FACES, liner_ref[...])
    fold_faces(0, FACES // 3)

    each_side(off_copy, "wait_recv", True)
    lane = iota((8, LANES), 1)
    offs = jnp.concatenate(
        [
            jnp.where(lane < elems, off_halo[0], pltpu.roll(off_send[...], elems, 1)),
            jnp.where(lane < elems, off_halo[1], 0.0),
        ],
        axis=1,
    )
    offs_col = jnp.concatenate([offs, jnp.zeros((LANES - 8, 2 * LANES), F32)], axis=0).T

    def picks(out_lo, count, in_lo):
        place = iota((count, LANES), 0) + (out_lo - in_lo) - iota((count, LANES), 1)
        place = place.astype(F32)
        cols = offs_col[out_lo : out_lo + count]
        here = offs if in_lo == 0 else pltpu.roll(offs, 2 * LANES - in_lo, 1)
        here = here[:, :LANES]

        def hot(x):
            return jnp.where(x, 1.0, 0.0).astype(BF16)

        fwd = [hot(place + cols[:, f : f + 1] == 0.0) for f in range(FACES)]
        adj = [hot(place == here[f : f + 1, :]) for f in range(FACES)]
        return fwd, adj

    half = (3 * elems - 2 * RIM) // 2
    for side in range(2):
        fwd, adj = picks(RIM + side * half, half, side * elems)
        for f in range(FACES):
            at = pl.ds((f % 2) * LANES, LANES)
            pick_fwd_ends[side, f // 2, :, at] = fwd[f]
            pick_adj_ends[side, f // 2, :, at] = adj[f]
    mid_rows = pick_fwd_mid.shape[1]
    mid_lo = elems - (mid_rows - elems) // 2
    fwd, adj = picks(mid_lo, mid_rows, elems // 2)
    for f in range(FACES):
        at = pl.ds((f % 2) * LANES, LANES)
        pick_fwd_mid[f // 2, :, at] = fwd[f]
        pick_adj_mid[f // 2, :, at] = adj[f]

    table = adm_send[...]
    for k in range(1, n):
        adm_copy(k).wait_recv()
        table = table + adm_recv[k - 1]
    face_all = offs_col[: 3 * elems, FACES : FACES + 1]
    weight = offs_col[elems : 2 * elems, FACES + 1 : FACES + 2]
    has_face = face_all == iota((3 * elems, faces), 1).astype(F32)
    y_re = jnp.sum(jnp.where(has_face, table[0:1], 0.0), axis=1, keepdims=True)
    y_im = jnp.sum(jnp.where(has_face, table[1:2], 0.0), axis=1, keepdims=True)
    own_face = offs_col[elems : 2 * elems, FACES : FACES + 1]
    own_face = own_face == iota((elems, faces), 1).astype(F32)

    admit_ref[0] = jnp.broadcast_to(y_re, (3 * elems, LANES))
    admit_ref[1] = jnp.broadcast_to(y_im, (3 * elems, LANES))
    admit_ref[2] = jnp.broadcast_to(-y_im, (3 * elems, LANES))
    split = nb // LANES * LANES

    def put(which, s, lo, value):
        count = value.shape[0]
        turned = swap(value)
        at, b = pl.ds(lo, count), s % 2
        is_re = iota((count, wide - split), 1) < nb - split

        def keep(ref, side, x):
            part = x[:, split:wide]
            if side == 0:
                ref[b, 0, at, 0:split] = x[:, :split].astype(BF16)
                ref[b, 0, at, split:wide] = jnp.where(is_re, part, 0.0).astype(BF16)
            else:
                ref[b, 1, at, split:wide] = jnp.where(is_re, 0.0, part).astype(BF16)
                ref[b, 1, at, wide:width] = x[:, wide:].astype(BF16)

        keep(field_re, 0, value)
        keep(field_re, 1, turned)
        keep(field_im, 0, turned)
        keep(field_im, 1, value)
        y_r = admit_ref[0, at]
        y_i = admit_ref[1 + which, at]
        for c in range(0, wide, LANES):
            re, im = value[:, c : c + LANES], turned[:, c : c + LANES]
            wall_re[b, at, c : c + LANES] = (y_r * re - y_i * im).astype(BF16)
            wall_im[b, at, c : c + LANES] = (y_r * im + y_i * re).astype(BF16)

    def rows_of(ref, spans):
        parts = [ref[lo:hi] for lo, hi in spans]
        return parts[0] if len(parts) == 1 else jnp.concatenate(parts, axis=0)

    def sweep(s, blocks, w_ref):
        b = (s - 1) % 2
        spans = [span for pieces, _ in blocks for _, _, span in pieces]

        parts = [[] for _ in range(FACES)]
        for pieces, taken in blocks:
            picked = [
                pick[i, lo - base : hi - base]
                for i in range(FACES // 2)
                for pick, base, (lo, hi) in pieces
            ]
            given = [
                jnp.concatenate([field[b, i, lo:hi] for i in range(2) for lo, hi in taken], axis=0)
                for field in (field_re, field_im)
            ]
            got = dot(jnp.concatenate(picked, axis=0), jnp.concatenate(given, axis=1)).astype(BF16)
            count = got.shape[0] // (FACES // 2)
            for i, part in enumerate(parts):
                row, lane = i % (FACES // 2) * count, i // (FACES // 2) * width
                part.append(got[row : row + count, lane : lane + width])
        met = [part[0] if len(part) == 1 else jnp.concatenate(part, axis=0) for part in parts]
        left = jnp.concatenate(
            [
                jnp.concatenate(met[: FACES // 2] + [rows_of(wall_re.at[b], spans)], axis=1),
                jnp.concatenate(met[FACES // 2 :] + [rows_of(wall_im.at[b], spans)], axis=1),
            ],
            axis=0,
        )
        prod = dot(left, w_ref[...])
        count = prod.shape[0] // 2
        rest = rows_of(start_ref, spans) - prod[:count]
        turned = swap(prod[count:])
        is_re = iota((count, wide - split), 1) < nb - split
        part = turned[:, split:wide]
        return jnp.concatenate(
            [
                rest[:, :split] + turned[:, :split],
                rest[:, split:wide] + jnp.where(is_re, part, -part),
                rest[:, wide:] - turned[:, wide:],
            ],
            axis=1,
        )

    def solve(which, start, ends, middle, w_ref, beside):
        ext[which, own] = start.astype(BF16)
        for reach in range(2):
            each_side(lambda side: halo_copy(which, reach, side), "start", False)
        start_ref[own] = start
        put(which, 0, elems, start)

        total = 3 * elems

        def lower(span):
            return (ends.at[0], RIM, span)

        def upper(span):
            return (ends.at[1], RIM + half, span)

        def centre(*spans):
            taken = (elems // 2, elems // 2 + LANES)
            return [(middle, mid_lo, span) for span in spans], [taken]

        def first_sweep(*blocks):
            now = sweep(1, blocks, w_ref)
            at = 0
            for lo, hi in [span for pieces, _ in blocks for _, _, span in pieces]:
                put(which, 1, lo, now[at : at + hi - lo])
                at += hi - lo

        def arrive(reach):
            each_side(lambda side: halo_copy(which, reach, side), "wait_recv", True)
            for lo in (elems // 2 * (1 - reach), 2 * elems + elems // 2 * reach):
                halo = ext[which, lo : lo + elems // 2].astype(F32)
                start_ref[lo : lo + elems // 2] = halo
                put(which, 0, lo, halo)

        inner, near_lo, far_lo = elems + RIM, elems // 2 + RIM, RIM
        beside()
        first_sweep(centre((inner, total - inner)))
        arrive(0)
        first_sweep(centre((near_lo, inner), (total - inner, total - near_lo)))
        arrive(1)
        outer = [lower((far_lo, near_lo)), upper((total - near_lo, total - far_lo))]
        first_sweep((outer, [(0, elems), (total - elems, total)]))
        for s in range(2, SWEEPS + 1):
            lo, hi = RIM * s, total - RIM * s
            if hi - lo > mid_rows:
                blocks = (
                    ([lower((lo, total // 2))], [(0, LANES)]),
                    ([upper((total // 2, hi))], [(total - LANES, total)]),
                )
            else:
                blocks = (centre((lo, hi)),)
            now = sweep(s, blocks, w_ref)
            if s < SWEEPS:
                put(which, s, lo, now)
        return now.astype(BF16)

    for j in (0, 1, 2):
        near_copy(j).wait_recv()
        forcing = forcing + near_recv[j].astype(F32)
    for t in range(1, quads):
        for h in range(pieces):
            far_copy(t, h).wait_recv()
        forcing = forcing + far_recv[t - 1].astype(F32)

    state = solve(
        0,
        dot(forcing.astype(BF16), inv_full[...]),
        pick_fwd_ends,
        pick_fwd_mid,
        w_fwd,
        lambda: fold_faces(FACES // 3, 2 * FACES // 3),
    )
    source = weight * state.astype(F32)

    def sent_halo(which):
        for reach in range(2):
            each_side(lambda side: halo_copy(which, reach, side), "wait_send", False)

    walls = []

    def beside():
        state_ref[...] = state
        walls.append(dot(state, liner_full[...]))
        fold_faces(2 * FACES // 3, FACES)
        for t in range(1, quads):
            for h in range(pieces):
                for j in range(QUAD - 1):
                    mid_copy(j, t, h).wait_send()
                far_copy(t, h).wait_send()
        for j in range(QUAD - 1):
            near_copy(j).wait_send()
        for k in range(1, n):
            adm_copy(k).wait_send()
        each_side(off_copy, "wait_send", False)
        sent_halo(0)

    adjoint = solve(
        1,
        dot(source.astype(BF16), inv_herm[...]),
        pick_adj_ends,
        pick_adj_mid,
        w_adj,
        beside,
    )
    adjoint_f = adjoint.astype(F32)
    wall = walls[0]
    term_re = jnp.sum(adjoint_f * wall, axis=1, keepdims=True) / -16.0
    term_im = jnp.sum(adjoint_f * times_i(wall), axis=1, keepdims=True) / -16.0
    grad_re = jnp.sum(jnp.where(own_face, term_re, 0.0), axis=0, keepdims=True)
    grad_im = jnp.sum(jnp.where(own_face, term_im, 0.0), axis=0, keepdims=True)
    total = jnp.concatenate([grad_re, grad_im, jnp.zeros((6, faces), F32)], axis=0)
    grad_send[...] = total
    for k in range(1, n):
        grad_copy(k).start()
    adjoint_ref[...] = adjoint
    for k in range(1, n):
        grad_copy(k).wait_recv()
        total = total + grad_recv[k - 1]
    total = jnp.where(mine_f, total, 0.0)
    parts = [total[:, i : i + LANES] for i in range(0, faces, LANES)]
    turned = pltpu.roll(sum(parts[1:], parts[0]), LANES - lax.rem(place, LANES), 1)
    grad_ref[...] = turned[0:2, 0:lin]

    for k in range(1, n):
        grad_copy(k).wait_send()
    sent_halo(1)


def finish(state_in, adjoint_in, grad_in, state_out, adjoint_out, grad_out, sems):
    pairs = ((state_in, state_out), (adjoint_in, adjoint_out), (grad_in, grad_out))
    moves = [pltpu.make_async_copy(a, b, sems.at[i]) for i, (a, b) in enumerate(pairs)]
    for move in moves:
        move.start()
    for move in moves:
        move.wait()


def solution(mesh):
    n = mesh.shape["mesh"]

    def local(
        src_rows,
        src_owner,
        src_slot,
        neighbour_offset,
        liner_face,
        admittance,
        observe_weight,
        coupling,
        block_inv,
        liner_op,
    ):
        rows, width = src_rows.shape
        nb = width // 2
        elems = liner_face.shape[0]
        lin = admittance.shape[1]
        faces = n * lin
        quads = n // QUAD
        pieces = 2
        wide = -(-nb // LANES) * LANES
        half = (3 * elems - 2 * RIM) // 2
        others = max(quads - 1, 1)
        vmem, dma = pltpu.VMEM, pltpu.SemaphoreType.DMA
        args = (
            src_owner.reshape(1, rows),
            src_slot.reshape(1, rows),
            neighbour_offset.T,
            liner_face.reshape(1, elems),
            admittance,
            observe_weight.reshape(1, elems),
            src_rows,
            coupling,
            block_inv,
            liner_op,
        )
        parts = pl.pallas_call(
            functools.partial(kernel, n),
            out_shape=(
                vmem((elems, width), BF16),
                vmem((elems, width), BF16),
                vmem((2, lin), F32),
            ),
            in_specs=[pl.BlockSpec(memory_space=pltpu.HBM)] * len(args),
            out_specs=(pl.BlockSpec(memory_space=pltpu.VMEM),) * 3,
            scratch_shapes=[vmem(x.shape, x.dtype) for x in args]
            + [
                dma((len(args),)),
                vmem((QUAD - 1, others, elems, width), BF16),
                vmem((QUAD - 1, elems, width), BF16),
                vmem((QUAD - 1, others, elems, width), BF16),
                vmem((others, pieces, elems // pieces, width), BF16),
                vmem((QUAD - 1, elems, width), BF16),
                vmem((others, elems, width), BF16),
                dma((2, QUAD - 1, others, pieces)),
                dma((2, QUAD - 1)),
                dma((2, others, pieces)),
                vmem((8, faces), F32),
                vmem((n - 1, 8, faces), F32),
                dma((2, n - 1)),
                vmem((8, LANES), F32),
                vmem((2, 8, LANES), F32),
                dma((2, 2)),
                vmem((8, faces), F32),
                vmem((n - 1, 8, faces), F32),
                dma((2, n - 1)),
                vmem((2, 3 * elems, width), BF16),
                dma((2, 2, 2, 2)),
                vmem((3 * elems, width), F32),
                vmem((2, 2, 3 * elems, width), BF16),
                vmem((2, 2, 3 * elems, width), BF16),
                vmem((2, 3 * elems, wide), BF16),
                vmem((2, 3 * elems, wide), BF16),
                vmem((width, width), BF16),
                vmem((width, width), BF16),
                vmem((width, width), BF16),
                vmem((FACES * nb + wide, width), BF16),
                vmem((FACES * nb + wide, width), BF16),
                vmem((2, FACES // 2, half, 2 * LANES), BF16),
                vmem((2, FACES // 2, half, 2 * LANES), BF16),
                vmem((FACES // 2, LANES - 2 * RIM, 2 * LANES), BF16),
                vmem((FACES // 2, LANES - 2 * RIM, 2 * LANES), BF16),
                vmem((3, 3 * elems, LANES), F32),
            ],
            compiler_params=pltpu.CompilerParams(
                collective_id=0, has_side_effects=True, vmem_limit_bytes=2**26 - 2**21
            ),
        )(*(pltpu.with_memory_space_constraint(x, pltpu.HBM) for x in args))
        anywhere = pl.BlockSpec(memory_space=pl.ANY)
        return tuple(
            pl.pallas_call(
                finish,
                out_shape=tuple(jax.ShapeDtypeStruct(x.shape, x.dtype) for x in parts),
                in_specs=[anywhere] * 3,
                out_specs=(anywhere,) * 3,
                scratch_shapes=[dma((3,))],
                compiler_params=pltpu.CompilerParams(vmem_limit_bytes=2**20),
            )(*parts)
        )

    placed = (
        P(("mode", "mesh"), None),
        P(("mode", "mesh"), None),
        P(("mode", "mesh")),
        P(("mode", "mesh"), None),
        P(("mode", "mesh")),
        P("mode", "mesh"),
        P(("mode", "mesh")),
        P("mode", None, None),
        P("mode", None),
        P("mode", None),
    )
    return jax.shard_map(
        local,
        mesh=mesh,
        in_specs=placed,
        out_specs=(P(("mode", "mesh"), None), P(("mode", "mesh"), None), P("mode", "mesh")),
        check_vma=False,
    )
```

```python
import functools

import jax
import jax.numpy as jnp
from jax import lax
from jax.experimental import pallas as pl
from jax.experimental.pallas import tpu as pltpu
from jax.sharding import PartitionSpec as P

SWEEPS = 4
RIM = 16
FACES = 6
QUAD = 4
LANES = 128
MESH = pl.DeviceIdType.MESH
F32 = jnp.float32
BF16 = jnp.bfloat16


def iota(shape, dim):
    return lax.broadcasted_iota(jnp.int32, shape, dim)


def dot(a, b):
    return jnp.dot(a, b, preferred_element_type=F32)


def swap(x):
    return pltpu.roll(x, x.shape[1] // 2, 1)


def first(x):
    return iota(x.shape, 1) < x.shape[1] // 2


def times_i(x):
    turned = swap(x)
    return jnp.where(first(x), -turned, turned)


def full(x):
    x = x.astype(F32)
    return jnp.concatenate([x, times_i(x)], axis=0)


def kernel(
    n,
    owner_hbm,
    slot_hbm,
    off_hbm,
    face_hbm,
    adm_hbm,
    weight_hbm,
    src_hbm,
    coupling_hbm,
    inv_hbm,
    liner_hbm,
    state_ref,
    adjoint_ref,
    grad_ref,
    owner_ref,
    slot_ref,
    off_ref,
    face_ref,
    adm_ref,
    weight_ref,
    src_ref,
    coupling_ref,
    inv_ref,
    liner_ref,
    load_sems,
    far_send,
    near_send,
    mid,
    summed,
    near_recv,
    far_recv,
    mid_sems,
    near_sems,
    far_sems,
    adm_send,
    adm_recv,
    adm_sems,
    off_send,
    off_halo,
    off_sems,
    grad_send,
    grad_recv,
    grad_sems,
    ext,
    halo_sems,
    start_ref,
    field_re,
    field_im,
    wall_re,
    wall_im,
    inv_full,
    inv_herm,
    liner_full,
    w_fwd,
    w_adj,
    pick_fwd_ends,
    pick_adj_ends,
    pick_fwd_mid,
    pick_adj_mid,
    admit_ref,
):
    me = lax.axis_index("mesh")
    elems = off_ref.shape[1]
    nb, width = inv_ref.shape
    lin = adm_ref.shape[1]
    rows = src_ref.shape[0]
    faces = adm_send.shape[1]
    wide = wall_re.shape[2]
    quads = n // QUAD
    pieces = summed.shape[1]
    piece = elems // pieces
    own = pl.ds(elems, elems)

    up, down = jnp.minimum(me + 1, n - 1), jnp.maximum(me - 1, 0)
    has_up, has_down = me < n - 1, me > 0

    barrier = pltpu.get_barrier_semaphore()
    for k in range(1, n):
        pl.semaphore_signal(
            barrier, inc=1, device_id={"mesh": lax.rem(me + k, n)}, device_id_type=MESH
        )

    loads = [
        pltpu.make_async_copy(hbm, here, load_sems.at[i])
        for i, (hbm, here) in enumerate(
            (
                (owner_hbm, owner_ref),
                (slot_hbm, slot_ref),
                (src_hbm, src_ref),
                (off_hbm, off_ref),
                (face_hbm, face_ref),
                (weight_hbm, weight_ref),
                (adm_hbm, adm_ref),
                (inv_hbm, inv_ref),
                (coupling_hbm, coupling_ref),
                (liner_hbm, liner_ref),
            )
        )
    ]
    for load in loads:
        load.start()

    def to(src, dst, sems, at, p):
        return pltpu.make_async_remote_copy(
            src_ref=src,
            dst_ref=dst,
            send_sem=sems.at[(0, *at)],
            recv_sem=sems.at[(1, *at)],
            device_id={"mesh": p},
            device_id_type=MESH,
        )

    q, r = me // QUAD, lax.rem(me, QUAD)
    high, low = r // 2, lax.rem(r, 2)
    near = [2 * high + 1 - low, 2 * (1 - high) + low, 2 * (1 - high) + 1 - low]

    def quad_at(t):
        return lax.rem(q + t, quads)

    def mid_copy(j, t, h):
        part = pl.ds(h * piece, piece)
        return to(
            far_send.at[j, t - 1, part],
            mid.at[j, t - 1, part],
            mid_sems,
            (j, t - 1, h),
            q * QUAD + near[j],
        )

    def near_copy(j):
        return to(near_send.at[j], near_recv.at[j], near_sems, (j,), q * QUAD + near[j])

    def far_copy(t, h):
        return to(
            summed.at[t - 1, h],
            far_recv.at[t - 1, pl.ds(h * piece, piece)],
            far_sems,
            (t - 1, h),
            quad_at(t) * QUAD + r,
        )

    def adm_copy(k):
        return to(adm_send, adm_recv.at[k - 1], adm_sems, (k - 1,), lax.rem(me + k, n))

    def grad_copy(k):
        return to(grad_send, grad_recv.at[k - 1], grad_sems, (k - 1,), lax.rem(me + k, n))

    def off_copy(side):
        return to(off_send, off_halo.at[side], off_sems, (side,), up if side == 0 else down)

    def halo_copy(solve, reach, side):
        mine = elems + (elems // 2 if (side == 0) == (reach == 0) else 0)
        there = mine - elems if side == 0 else mine + elems
        return to(
            ext.at[solve, pl.ds(mine, elems // 2)],
            ext.at[solve, pl.ds(there, elems // 2)],
            halo_sems,
            (solve, reach, side),
            up if side == 0 else down,
        )

    def each_side(copy, what, incoming):
        @pl.when(has_down if incoming else has_up)
        def _():
            getattr(copy(0), what)()

        @pl.when(has_up if incoming else has_down)
        def _():
            getattr(copy(1), what)()

    @pl.when(jnp.logical_not(has_down))
    def _():
        off_halo[0] = jnp.zeros((8, LANES), F32)
        for solve in range(2):
            ext[solve, 0:elems] = jnp.zeros((elems, width), BF16)

    @pl.when(jnp.logical_not(has_up))
    def _():
        off_halo[1] = jnp.zeros((8, LANES), F32)
        for solve in range(2):
            ext[solve, 2 * elems : 3 * elems] = jnp.zeros((elems, width), BF16)

    field_re[...] = jnp.zeros_like(field_re)
    field_im[...] = jnp.zeros_like(field_im)
    for load in loads[:3]:
        load.wait()
    target = owner_ref[...] * elems + slot_ref[...]

    def partial_sums(owners):
        picks = [(iota((elems, rows), 0) + p * elems) == target for p in owners]
        picks = [pick.astype(F32).astype(BF16) for pick in picks]
        got = dot(jnp.concatenate(picks, axis=0), src_ref[...])
        return [got[i * elems : (i + 1) * elems] for i in range(len(owners))]

    for t in range(1, quads):
        got = partial_sums([quad_at(t) * QUAD + near[j] for j in range(QUAD - 1)])
        for j in range(QUAD - 1):
            far_send[j, t - 1] = got[j].astype(BF16)

    depth = w_fwd.shape[0]
    over = depth - (FACES + 1) * nb

    def fold_forward():
        for load in loads[7:]:
            load.wait()
        inv_full[...] = full(inv_ref[...]).astype(BF16)

        @pl.loop(0, FACES)
        def _(f):
            at = pl.ds(pl.multiple_of(f * nb, nb), nb)
            w_fwd[at, :] = dot(coupling_ref[f], inv_full[...]).astype(BF16)

        w_fwd[FACES * nb : depth - over, :] = dot(liner_ref[...], inv_full[...]).astype(BF16)
        w_fwd[depth - over :, :] = jnp.zeros((over, width), BF16)
        w_adj[depth - over :, :] = jnp.zeros((over, width), BF16)

    sends_first = lax.rem(lax.axis_index("mode"), 2) == 0

    pl.semaphore_wait(barrier, n - 1)
    for h in range(pieces):
        for t in range(1, quads):
            for j in (2, 0, 1):
                mid_copy(j, t, h).start()
    got = partial_sums([q * QUAD + near[j] for j in range(QUAD - 1)])
    for j in range(QUAD - 1):
        near_send[j] = got[j].astype(BF16)
    near_copy(2).start()
    near_copy(0).start()
    for load in loads[3:7]:
        load.wait()
    off_send[...] = jnp.zeros_like(off_send)
    off_send[0:FACES, 0:elems] = off_ref[...].astype(F32)
    off_send[FACES : FACES + 1, 0:elems] = face_ref[...].astype(F32)
    off_send[FACES + 1 : FACES + 2, 0:elems] = weight_ref[...]
    adm_send[...] = jnp.zeros_like(adm_send)
    adm_send[0:2, 0:lin] = adm_ref[...]
    place = me * lin
    turned = pltpu.roll(adm_send[:, :LANES], lax.rem(place, LANES), 1)
    lane_f = iota((8, faces), 1)
    mine_f = jnp.logical_and(lane_f >= place, lane_f < place + lin)
    adm_send[...] = jnp.where(
        mine_f, jnp.concatenate([turned] * (faces // LANES), axis=1), 0.0
    )

    each_side(off_copy, "start", False)
    for k in range(1, n):
        adm_copy(k).start()
    fold_forward()

    forcing, *far_own = partial_sums([me] + [quad_at(t) * QUAD + r for t in range(1, quads)])
    for h in range(pieces):
        for t in range(1, quads):
            total = far_own[t - 1][h * piece : (h + 1) * piece]
            for j in (2, 0, 1):
                mid_copy(j, t, h).wait_recv()
                total = total + mid[j, t - 1, h * piece : (h + 1) * piece].astype(F32)
            summed[t - 1, h] = total.astype(BF16)
            far_copy(t, h).start()
    near_copy(1).start()

    def fold_adjoint(f, matrix):
        turned = dot(inv_ref[...], full(matrix).astype(BF16))
        turned = jnp.concatenate([turned, jnp.zeros((wide - nb, width), F32)], axis=0).T
        rest = jnp.zeros((nb, width - wide), F32)
        re = jnp.concatenate([turned[:nb], rest], axis=1)
        im = jnp.concatenate([turned[nb:], rest], axis=1)
        at = pl.ds(f * nb if isinstance(f, int) else pl.multiple_of(f * nb, nb), nb)
        w_adj[at, :] = (re - swap(im)).astype(BF16)

    def fold_faces(begin, end):
        @pl.loop(begin, end)
        def _(f):
            fold_adjoint(f, coupling_ref[f])

    inv_herm[...] = full(inv_ref[...]).T.astype(BF16)
    liner_full[...] = full(liner_ref[...]).astype(BF16)
    fold_adjoint(FACES, liner_ref[...])
    fold_faces(0, FACES // 3)

    each_side(off_copy, "wait_recv", True)
    lane = iota((8, LANES), 1)
    offs = jnp.concatenate(
        [
            jnp.where(lane < elems, off_halo[0], pltpu.roll(off_send[...], elems, 1)),
            jnp.where(lane < elems, off_halo[1], 0.0),
        ],
        axis=1,
    )
    offs_col = jnp.concatenate([offs, jnp.zeros((LANES - 8, 2 * LANES), F32)], axis=0).T

    def picks(out_lo, count, in_lo):
        place = iota((count, LANES), 0) + (out_lo - in_lo) - iota((count, LANES), 1)
        place = place.astype(F32)
        cols = offs_col[out_lo : out_lo + count]
        here = offs if in_lo == 0 else pltpu.roll(offs, 2 * LANES - in_lo, 1)
        here = here[:, :LANES]

        def hot(x):
            return jnp.where(x, 1.0, 0.0).astype(BF16)

        fwd = [hot(place + cols[:, f : f + 1] == 0.0) for f in range(FACES)]
        adj = [hot(place == here[f : f + 1, :]) for f in range(FACES)]
        return fwd, adj

    half = (3 * elems - 2 * RIM) // 2
    for side in range(2):
        fwd, adj = picks(RIM + side * half, half, side * elems)
        for f in range(FACES):
            at = pl.ds((f % 2) * LANES, LANES)
            pick_fwd_ends[side, f // 2, :, at] = fwd[f]
            pick_adj_ends[side, f // 2, :, at] = adj[f]
    mid_rows = pick_fwd_mid.shape[1]
    mid_lo = elems - (mid_rows - elems) // 2
    fwd, adj = picks(mid_lo, mid_rows, elems // 2)
    for f in range(FACES):
        at = pl.ds((f % 2) * LANES, LANES)
        pick_fwd_mid[f // 2, :, at] = fwd[f]
        pick_adj_mid[f // 2, :, at] = adj[f]

    table = adm_send[...]
    for k in range(1, n):
        adm_copy(k).wait_recv()
        table = table + adm_recv[k - 1]
    face_all = offs_col[: 3 * elems, FACES : FACES + 1]
    weight = offs_col[elems : 2 * elems, FACES + 1 : FACES + 2]
    has_face = face_all == iota((3 * elems, faces), 1).astype(F32)
    y_re = jnp.sum(jnp.where(has_face, table[0:1], 0.0), axis=1, keepdims=True)
    y_im = jnp.sum(jnp.where(has_face, table[1:2], 0.0), axis=1, keepdims=True)
    own_face = offs_col[elems : 2 * elems, FACES : FACES + 1]
    own_face = own_face == iota((elems, faces), 1).astype(F32)

    admit_ref[0] = jnp.broadcast_to(y_re, (3 * elems, LANES))
    admit_ref[1] = jnp.broadcast_to(y_im, (3 * elems, LANES))
    admit_ref[2] = jnp.broadcast_to(-y_im, (3 * elems, LANES))
    split = nb // LANES * LANES

    def put(which, s, lo, value):
        count = value.shape[0]
        turned = swap(value)
        at, b = pl.ds(lo, count), s % 2
        is_re = iota((count, wide - split), 1) < nb - split

        def keep(ref, side, x):
            part = x[:, split:wide]
            if side == 0:
                ref[b, 0, at, 0:split] = x[:, :split].astype(BF16)
                ref[b, 0, at, split:wide] = jnp.where(is_re, part, 0.0).astype(BF16)
            else:
                ref[b, 1, at, split:wide] = jnp.where(is_re, 0.0, part).astype(BF16)
                ref[b, 1, at, wide:width] = x[:, wide:].astype(BF16)

        keep(field_re, 0, value)
        keep(field_re, 1, turned)
        keep(field_im, 0, turned)
        keep(field_im, 1, value)
        y_r = admit_ref[0, at]
        y_i = admit_ref[1 + which, at]
        for c in range(0, wide, LANES):
            re, im = value[:, c : c + LANES], turned[:, c : c + LANES]
            wall_re[b, at, c : c + LANES] = (y_r * re - y_i * im).astype(BF16)
            wall_im[b, at, c : c + LANES] = (y_r * im + y_i * re).astype(BF16)

    def rows_of(ref, spans):
        parts = [ref[lo:hi] for lo, hi in spans]
        return parts[0] if len(parts) == 1 else jnp.concatenate(parts, axis=0)

    def sweep(s, blocks, w_ref):
        b = (s - 1) % 2
        spans = [span for pieces, _ in blocks for _, _, span in pieces]

        parts = [[] for _ in range(FACES)]
        for pieces, taken in blocks:
            picked = [
                pick[i, lo - base : hi - base]
                for i in range(FACES // 2)
                for pick, base, (lo, hi) in pieces
            ]
            given = [
                jnp.concatenate([field[b, i, lo:hi] for i in range(2) for lo, hi in taken], axis=0)
                for field in (field_re, field_im)
            ]
            got = dot(jnp.concatenate(picked, axis=0), jnp.concatenate(given, axis=1)).astype(BF16)
            count = got.shape[0] // (FACES // 2)
            for i, part in enumerate(parts):
                row, lane = i % (FACES // 2) * count, i // (FACES // 2) * width
                part.append(got[row : row + count, lane : lane + width])
        met = [part[0] if len(part) == 1 else jnp.concatenate(part, axis=0) for part in parts]
        left = jnp.concatenate(
            [
                jnp.concatenate(met[: FACES // 2] + [rows_of(wall_re.at[b], spans)], axis=1),
                jnp.concatenate(met[FACES // 2 :] + [rows_of(wall_im.at[b], spans)], axis=1),
            ],
            axis=0,
        )
        prod = dot(left, w_ref[...])
        count = prod.shape[0] // 2
        rest = rows_of(start_ref, spans) - prod[:count]
        turned = swap(prod[count:])
        is_re = iota((count, wide - split), 1) < nb - split
        part = turned[:, split:wide]
        return jnp.concatenate(
            [
                rest[:, :split] + turned[:, :split],
                rest[:, split:wide] + jnp.where(is_re, part, -part),
                rest[:, wide:] - turned[:, wide:],
            ],
            axis=1,
        )

    def solve(which, start, ends, middle, w_ref, beside):
        ext[which, own] = start.astype(BF16)
        for reach in range(2):
            each_side(lambda side: halo_copy(which, reach, side), "start", False)
        start_ref[own] = start
        put(which, 0, elems, start)

        total = 3 * elems

        def lower(span):
            return (ends.at[0], RIM, span)

        def upper(span):
            return (ends.at[1], RIM + half, span)

        def centre(*spans):
            taken = (elems // 2, elems // 2 + LANES)
            return [(middle, mid_lo, span) for span in spans], [taken]

        def first_sweep(*blocks):
            now = sweep(1, blocks, w_ref)
            at = 0
            for lo, hi in [span for pieces, _ in blocks for _, _, span in pieces]:
                put(which, 1, lo, now[at : at + hi - lo])
                at += hi - lo

        def arrive(reach):
            each_side(lambda side: halo_copy(which, reach, side), "wait_recv", True)
            for lo in (elems // 2 * (1 - reach), 2 * elems + elems // 2 * reach):
                halo = ext[which, lo : lo + elems // 2].astype(F32)
                start_ref[lo : lo + elems // 2] = halo
                put(which, 0, lo, halo)

        inner, near_lo, far_lo = elems + RIM, elems // 2 + RIM, RIM
        beside()
        first_sweep(centre((inner, total - inner)))
        arrive(0)
        first_sweep(centre((near_lo, inner), (total - inner, total - near_lo)))
        arrive(1)
        outer = [lower((far_lo, near_lo)), upper((total - near_lo, total - far_lo))]
        first_sweep((outer, [(0, elems), (total - elems, total)]))
        for s in range(2, SWEEPS + 1):
            lo, hi = RIM * s, total - RIM * s
            if hi - lo > mid_rows:
                blocks = (
                    ([lower((lo, total // 2))], [(0, LANES)]),
                    ([upper((total // 2, hi))], [(total - LANES, total)]),
                )
            else:
                blocks = (centre((lo, hi)),)
            now = sweep(s, blocks, w_ref)
            if s < SWEEPS:
                put(which, s, lo, now)
        return now.astype(BF16)

    for j in (0, 1, 2):
        near_copy(j).wait_recv()
        forcing = forcing + near_recv[j].astype(F32)
    for t in range(1, quads):
        for h in range(pieces):
            far_copy(t, h).wait_recv()
        forcing = forcing + far_recv[t - 1].astype(F32)

    state = solve(
        0,
        dot(forcing.astype(BF16), inv_full[...]),
        pick_fwd_ends,
        pick_fwd_mid,
        w_fwd,
        lambda: fold_faces(FACES // 3, 2 * FACES // 3),
    )
    source = weight * state.astype(F32)

    def sent_halo(which):
        for reach in range(2):
            each_side(lambda side: halo_copy(which, reach, side), "wait_send", False)

    walls = []

    def beside():
        state_ref[...] = state
        walls.append(dot(state, liner_full[...]))
        fold_faces(2 * FACES // 3, FACES)
        for t in range(1, quads):
            for h in range(pieces):
                for j in range(QUAD - 1):
                    mid_copy(j, t, h).wait_send()
                far_copy(t, h).wait_send()
        for j in range(QUAD - 1):
            near_copy(j).wait_send()
        for k in range(1, n):
            adm_copy(k).wait_send()
        each_side(off_copy, "wait_send", False)
        sent_halo(0)

    adjoint = solve(
        1,
        dot(source.astype(BF16), inv_herm[...]),
        pick_adj_ends,
        pick_adj_mid,
        w_adj,
        beside,
    )
    adjoint_f = adjoint.astype(F32)
    wall = walls[0]
    term_re = jnp.sum(adjoint_f * wall, axis=1, keepdims=True) / -16.0
    term_im = jnp.sum(adjoint_f * times_i(wall), axis=1, keepdims=True) / -16.0
    grad_re = jnp.sum(jnp.where(own_face, term_re, 0.0), axis=0, keepdims=True)
    grad_im = jnp.sum(jnp.where(own_face, term_im, 0.0), axis=0, keepdims=True)
    total = jnp.concatenate([grad_re, grad_im, jnp.zeros((6, faces), F32)], axis=0)
    grad_send[...] = total
    for k in range(1, n):
        grad_copy(k).start()
    adjoint_ref[...] = adjoint
    for k in range(1, n):
        grad_copy(k).wait_recv()
        total = total + grad_recv[k - 1]
    total = jnp.where(mine_f, total, 0.0)
    parts = [total[:, i : i + LANES] for i in range(0, faces, LANES)]
    turned = pltpu.roll(sum(parts[1:], parts[0]), LANES - lax.rem(place, LANES), 1)
    grad_ref[...] = turned[0:2, 0:lin]

    for k in range(1, n):
        grad_copy(k).wait_send()
    sent_halo(1)


def finish(state_in, adjoint_in, grad_in, state_out, adjoint_out, grad_out, sems):
    pairs = ((state_in, state_out), (adjoint_in, adjoint_out), (grad_in, grad_out))
    moves = [pltpu.make_async_copy(a, b, sems.at[i]) for i, (a, b) in enumerate(pairs)]
    for move in moves:
        move.start()
    for move in moves:
        move.wait()


def solution(mesh):
    n = mesh.shape["mesh"]

    def local(
        src_rows,
        src_owner,
        src_slot,
        neighbour_offset,
        liner_face,
        admittance,
        observe_weight,
        coupling,
        block_inv,
        liner_op,
    ):
        rows, width = src_rows.shape
        nb = width // 2
        elems = liner_face.shape[0]
        lin = admittance.shape[1]
        faces = n * lin
        quads = n // QUAD
        pieces = 2
        wide = -(-nb // LANES) * LANES
        half = (3 * elems - 2 * RIM) // 2
        others = max(quads - 1, 1)
        vmem, dma = pltpu.VMEM, pltpu.SemaphoreType.DMA
        args = (
            src_owner.reshape(1, rows),
            src_slot.reshape(1, rows),
            neighbour_offset.T,
            liner_face.reshape(1, elems),
            admittance,
            observe_weight.reshape(1, elems),
            src_rows,
            coupling,
            block_inv,
            liner_op,
        )
        parts = pl.pallas_call(
            functools.partial(kernel, n),
            out_shape=(
                vmem((elems, width), BF16),
                vmem((elems, width), BF16),
                vmem((2, lin), F32),
            ),
            in_specs=[pl.BlockSpec(memory_space=pltpu.HBM)] * len(args),
            out_specs=(pl.BlockSpec(memory_space=pltpu.VMEM),) * 3,
            scratch_shapes=[vmem(x.shape, x.dtype) for x in args]
            + [
                dma((len(args),)),
                vmem((QUAD - 1, others, elems, width), BF16),
                vmem((QUAD - 1, elems, width), BF16),
                vmem((QUAD - 1, others, elems, width), BF16),
                vmem((others, pieces, elems // pieces, width), BF16),
                vmem((QUAD - 1, elems, width), BF16),
                vmem((others, elems, width), BF16),
                dma((2, QUAD - 1, others, pieces)),
                dma((2, QUAD - 1)),
                dma((2, others, pieces)),
                vmem((8, faces), F32),
                vmem((n - 1, 8, faces), F32),
                dma((2, n - 1)),
                vmem((8, LANES), F32),
                vmem((2, 8, LANES), F32),
                dma((2, 2)),
                vmem((8, faces), F32),
                vmem((n - 1, 8, faces), F32),
                dma((2, n - 1)),
                vmem((2, 3 * elems, width), BF16),
                dma((2, 2, 2, 2)),
                vmem((3 * elems, width), F32),
                vmem((2, 2, 3 * elems, width), BF16),
                vmem((2, 2, 3 * elems, width), BF16),
                vmem((2, 3 * elems, wide), BF16),
                vmem((2, 3 * elems, wide), BF16),
                vmem((width, width), BF16),
                vmem((width, width), BF16),
                vmem((width, width), BF16),
                vmem((FACES * nb + wide, width), BF16),
                vmem((FACES * nb + wide, width), BF16),
                vmem((2, FACES // 2, half, 2 * LANES), BF16),
                vmem((2, FACES // 2, half, 2 * LANES), BF16),
                vmem((FACES // 2, LANES - 2 * RIM, 2 * LANES), BF16),
                vmem((FACES // 2, LANES - 2 * RIM, 2 * LANES), BF16),
                vmem((3, 3 * elems, LANES), F32),
            ],
            compiler_params=pltpu.CompilerParams(
                collective_id=0, has_side_effects=True, vmem_limit_bytes=2**26 - 2**21
            ),
        )(*(pltpu.with_memory_space_constraint(x, pltpu.HBM) for x in args))
        anywhere = pl.BlockSpec(memory_space=pl.ANY)
        return tuple(
            pl.pallas_call(
                finish,
                out_shape=tuple(jax.ShapeDtypeStruct(x.shape, x.dtype) for x in parts),
                in_specs=[anywhere] * 3,
                out_specs=(anywhere,) * 3,
                scratch_shapes=[dma((3,))],
                compiler_params=pltpu.CompilerParams(vmem_limit_bytes=2**20),
            )(*parts)
        )

    placed = (
        P(("mode", "mesh"), None),
        P(("mode", "mesh"), None),
        P(("mode", "mesh")),
        P(("mode", "mesh"), None),
        P(("mode", "mesh")),
        P("mode", "mesh"),
        P(("mode", "mesh")),
        P("mode", None, None),
        P("mode", None),
        P("mode", None),
    )
    return jax.shard_map(
        local,
        mesh=mesh,
        in_specs=placed,
        out_specs=(P(("mode", "mesh"), None), P(("mode", "mesh"), None), P("mode", "mesh")),
        check_vma=False,
    )
```
